256 devices in a mesh: seq: 32 (over x, z_lo, core), mp: 8 (over z_hi, y).
Axes of the slice: x: 4, y: 4, z: 8 (z_hi: 2, z_lo: 4; z = z_hi * 4 + z_lo), core: 2. Of those that a mesh axis runs over, the one named last changes fastest.
Arguments:
- tokens: bfloat16 [16384, 4096], P('seq'), may hold values from -6 to 6
- in_weight: bfloat16 [3, 4096, 4096], P(None, 'seq', 'mp'), may hold values from -0.09375 to 0.09375
- short_filter: float32 [3, 7, 4096], P(None, None, 'mp'), may hold values from -2.4 to 2.4
- residues: float32 [4096, 16], P('mp'), may hold values from -2.1 to 2.1
- rates: float32 [4096, 16], P('mp'), may hold values from 3.0517578e-05 to 0.05
- skip: float32 [4096], P('mp'), may hold values from -4 to 4
Outputs:
- mixed: bfloat16 [16384, 4096], P('seq', 'mp')
The draws below stay inside these ranges and needn't reach their ends.
All inputs are finite; a program needn't handle non-finite values.
Results may differ from the reference program's by a relative error of at most 0.0065.
Values may be sent and summed in bfloat16 or wider, within the bound.
No kernel may reach another device: no remote copies, remote signals or barrier semaphores. Data moves between devices by JAX's collectives and lax.ppermute only.
A program may use at most 128 MiB of HBM per device.

```python
import math
import jax
import jax.numpy as jnp
from jax import lax

D = 4096
C = 4096
ORDER = 16
SHORT = 7
TOKENS = 16384


def steps_of(stream_key, extent, split, least, largest):
    level, own = 1.0, jax.random.fold_in(stream_key, 6)
    for axis_at, shards_of in split:
        heights = jnp.exp(jax.random.uniform(jax.random.fold_in(own, axis_at), (shards_of,), jnp.float32, least / len(split), largest / len(split)))
        level = level * jnp.repeat(heights, extent[axis_at] // shards_of).reshape([-1 if axis == axis_at else 1 for axis in range(len(extent))])
    return level


def noise(key, dims, spread, most, cuts=(), kind=jnp.bfloat16):
    level = steps_of(key, dims, cuts, -0.22, 0.18) if cuts else 1.0
    result = jax.random.normal(key, dims, jnp.float32) * spread * level
    return jnp.minimum(jnp.maximum(result, -most), most).astype(kind)


def setup_inputs(seed: int = 0) -> dict:
    splits = jax.random.split(jax.random.key(seed), 7)
    return {
        "tokens": noise(splits[0], (TOKENS, D), 1.0, 6.0, ((0, 32),)),
        "in_weight": noise(splits[1], (3, D, C), D ** -0.5, 0.09375, ((1, 32), (2, 8))),
        "short_filter": noise(splits[2], (3, SHORT, C), 0.4, 2.4, ((2, 8),), jnp.float32),
        "residues": noise(splits[3], (C, ORDER), 0.35, 2.1, ((0, 8),), jnp.float32),
        "rates": jnp.clip(jnp.exp(math.log(0.05) - 7.4014754 * jax.random.uniform(splits[4], (C, ORDER), jnp.float32) ** steps_of(splits[4], (C, ORDER), ((0, 8),), -0.2, 0.2)), 3.0517578125e-05, 0.05),
        "skip": noise(splits[5], (C,), 0.7, 4.0, ((0, 8),), jnp.float32),
    }


def filter_values(amplitudes, decays, length):
    positions = jnp.arange(length, dtype=jnp.float32)[:, None]
    total = jnp.zeros((length, amplitudes.shape[0]), jnp.float32)
    for which in range(ORDER):
        scale = amplitudes[:, which] * jnp.sqrt(-jnp.expm1(-2.0 * decays[:, which]))
        total = total + scale[None, :] * jnp.exp(-positions * decays[:, which][None, :])
    return total

def reference(tokens, in_weight, short_filter, residues, rates, skip):
    width = in_weight.shape[2]
    block = math.gcd(width, 512)
    count = width // block
    weights = in_weight.reshape(3, D, count, block).transpose(2, 0, 1, 3)
    taps = short_filter.reshape(3, SHORT, count, block).transpose(2, 0, 1, 3)
    amplitude_blocks = residues.reshape(count, block, ORDER)
    decay_blocks = rates.reshape(count, block, ORDER)
    skip_blocks = skip.reshape(count, block)

    def one_block(operands):
        weight_block, tap_block, amplitudes, decays, direct = operands
        projected = jnp.stack([jnp.dot(tokens, weight_block[s], preferred_element_type=jnp.float32) for s in range(3)])
        projected = lax.optimization_barrier(projected.astype(jnp.bfloat16)).astype(jnp.float32)
        padded = jnp.pad(projected, ((0, 0), (SHORT - 1, 0), (0, 0)))
        features = jnp.zeros_like(projected)
        for offset in range(SHORT):
            start = SHORT - 1 - offset
            features = features + tap_block[:, offset, None, :] * padded[:, start:start + TOKENS, :]
        signal = features[1] * features[2]
        filt = filter_values(amplitudes, decays, TOKENS)
        points = 2 * TOKENS
        spectrum = jnp.fft.rfft(signal, n=points, axis=0) * jnp.fft.rfft(filt, n=points, axis=0)
        conv = jnp.fft.irfft(spectrum, n=points, axis=0)[:TOKENS]
        return (features[0] * (conv + direct[None, :] * signal)).astype(jnp.bfloat16)
    outputs = lax.map(one_block, (weights, taps, amplitude_blocks, decay_blocks, skip_blocks))
    return outputs.transpose(1, 0, 2).reshape(TOKENS, C)
```

```python
import functools
import math

import jax
import jax.numpy as jnp
from jax import lax
from jax.experimental import pallas as pl
from jax.experimental.pallas import tpu as pltpu
from jax.sharding import PartitionSpec as P

SHORT = 7
X, Z, CORES = 4, 4, 2
CHIPS = X * Z
HALO = 16
LANES = 128
SEGMENTS = 8

ANY = pl.BlockSpec(memory_space=pl.ANY)
VMEM = pl.BlockSpec(memory_space=pltpu.VMEM)
SMEM = pl.BlockSpec(memory_space=pltpu.SMEM)


def place(x, z, core):
    return (x * Z + z) * CORES + core


def permute(value, target):
    pairs = []
    for x in range(X):
        for z in range(Z):
            for core in range(CORES):
                to = target(x, z, core)
                if to is not None:
                    pairs.append((place(x, z, core), place(*to)))
    return lax.ppermute(value, "seq", pairs)


def along_x(value, steps):
    return permute(value, lambda x, z, core: ((x + steps) % X, z, core))


def along_z(value, steps):
    return permute(value, lambda x, z, core: (x, (z + steps) % Z, core))


def swap_cores(value):
    return permute(value, lambda x, z, core: (x, z, 1 - core))


def next_chip(value):
    def target(x, z, core):
        chip = x * Z + z + 1
        return (chip // Z, chip % Z, core) if chip < CHIPS else None

    return permute(value, target)


def together(*values):
    return lax.optimization_barrier(values)


def gather_chips(block):
    half = block.shape[1] // 2
    up, down = along_z(block, 1), along_z(block, 3)
    right, left = along_x(block, 1), along_x(block, 3)
    up, right, left = together(up, right, left)
    (held, _) = together(block, up)
    across = along_z(held, 2)
    pieces = [(0, 0, 0, block), (1, 0, 0, right), (3, 0, 0, left)]
    previous = (0, right, left)
    for steps, source in ((1, up), (3, down), (2, across)):
        before, right, left = previous
        far_right = along_x(right[:, :half], 1)
        far_left = along_x(left[:, half:], 3)
        right, left = along_x(source, 1), along_x(source, 3)
        if steps == 1:
            right, left, far_right, far_left, down = together(right, left, far_right, far_left, down)
        elif steps == 3:
            right, left, far_right, far_left, across = together(
                right, left, far_right, far_left, across
            )
        else:
            right, left, far_right, far_left = together(right, left, far_right, far_left)
        pieces += [(2, before, 0, far_right), (2, before, half, far_left)]
        source = {1: up, 3: down, 2: across}[steps]
        pieces += [(0, steps, 0, source), (1, steps, 0, right), (3, steps, 0, left)]
        previous = (steps, right, left)
    before, right, left = previous
    pieces += [
        (2, before, 0, along_x(right[:, :half], 1)),
        (2, before, half, along_x(left[:, half:], 3)),
    ]
    return pieces


def rounded(value):
    return value.astype(jnp.bfloat16).astype(jnp.float32)


def signal_kernel(
    plan, where, *refs
):
    count = len(plan)
    pieces = refs[:count]
    mine, other, halo, taps, decay, amplitude, power = refs[count : count + 7]
    signal, start_conv, before, ends = refs[count + 7 : count + 11]
    rows, weights, key, value, sems = refs[count + 11 :]
    x, z, core = where[0], where[1], where[2]
    length, depth = mine.shape
    channels = weights.shape[2]
    steps = 2 * length // SEGMENTS
    order = ((HALO, mine, core), (HALO, other, 1 - core))
    copies = []
    offset = 0
    for at, (x_steps, z_steps, row, height) in enumerate(plan):
        chip = (x - x_steps + X) % X * Z + (z - z_steps + Z) % Z
        column = pl.multiple_of(chip * (depth // CHIPS) + row, LANES)
        group = [
            pltpu.make_async_copy(
                pieces[at], weights.at[:, pl.ds(offset, height), :], sems.at[at, 0]
            ),
            pltpu.make_async_copy(
                halo.at[:, pl.ds(column, height)],
                rows.at[pl.ds(0, HALO), pl.ds(offset, height)],
                sems.at[at, 1],
            ),
        ]
        for which, (first, array, block) in enumerate(order):
            group.append(
                pltpu.make_async_copy(
                    array.at[:, pl.ds(column, height)],
                    rows.at[
                        pl.ds(pl.multiple_of(first + block * length, HALO), length),
                        pl.ds(offset, height),
                    ],
                    sems.at[at, 2 + which],
                )
            )
        for copy in group:
            copy.start()
        copies.append((offset, height, group))
        offset += height
    parts = 4
    for part in range(parts):
        low, high = part * depth // parts, (part + 1) * depth // parts
        for offset, height, group in copies:
            if low <= offset < high:
                for copy in group:
                    copy.wait()
        last = part == parts - 1
        for stream, total in ((0, key), (1, value)):
            product = jnp.dot(
                rows[:, low:high], weights[stream, low:high, :], preferred_element_type=jnp.float32
            )
            for group in range(channels // LANES):
                share = product[:, group * LANES : (group + 1) * LANES]
                if part > 0:
                    share = total[group] + share
                total[group] = rounded(share) if last else share
    for low in range(0, channels, LANES):
        lanes = pl.ds(low, LANES)
        group = low // LANES

        def spread(ref, *index):
            return jnp.broadcast_to(ref[(*index, lanes)].reshape(1, LANES), (SEGMENTS, LANES))

        def load(ref, step):
            return ref[group, pl.ds(HALO + step, SEGMENTS, stride=steps), :]

        key_taps = [spread(taps, 1, offset) for offset in range(SHORT)]
        value_taps = [spread(taps, 2, offset) for offset in range(SHORT)]

        def featurize(step, carry):
            keys, values = carry
            keys = (load(key, step),) + keys
            values = (load(value, step),) + values
            total_key = key_taps[0] * keys[0]
            total_value = value_taps[0] * values[0]
            for offset in range(1, SHORT):
                total_key += key_taps[offset] * keys[offset]
                total_value += value_taps[offset] * values[offset]
            signal[step, :, lanes] = total_key * total_value
            return keys[:-1], values[:-1]

        lax.fori_loop(
            0,
            steps,
            featurize,
            (
                tuple(load(key, -offset) for offset in range(1, SHORT)),
                tuple(load(value, -offset) for offset in range(1, SHORT)),
            ),
            unroll=4,
        )
        modes = decay.shape[0]
        decays = [spread(decay, mode) for mode in range(modes)]
        amplitudes = [spread(amplitude, mode) for mode in range(modes)]

        def scan(step, states):
            here = signal[step, :, lanes]
            states = tuple(decays[mode] * states[mode] + here for mode in range(modes))
            terms = [amplitudes[mode] * states[mode] for mode in range(modes)]
            while len(terms) > 1:
                terms = [terms[at] + terms[at + 1] for at in range(0, len(terms), 2)]
            start_conv[step, :, lanes] = terms[0]
            return states

        empty = jnp.zeros((SEGMENTS, LANES), jnp.float32)
        states = lax.fori_loop(0, steps, scan, (empty,) * modes, unroll=2)
        segment = lax.broadcasted_iota(jnp.int32, (SEGMENTS, LANES), 0)
        for mode in range(modes):
            state = states[mode]
            for level, distance in enumerate((1, 2, 4)):
                moved = pltpu.roll(state, distance, 0)
                state = state + jnp.where(
                    segment >= distance, spread(power, level, mode) * moved, 0.0
                )
            before[mode, :, lanes] = jnp.where(segment >= 1, pltpu.roll(state, 1, 0), 0.0)
            ends[pl.ds(mode, 1), lanes] = state[SEGMENTS - 1 :, :]


def signals(where, pieces, mine, other, halo, taps, decay, amplitude, power):
    plan = tuple((x_steps, z_steps, row, array.shape[1]) for x_steps, z_steps, row, array in pieces)
    arrays = [array for _, _, _, array in pieces]
    length, depth = mine.shape
    modes, channels = decay.shape
    steps = 2 * length // SEGMENTS
    shape = jax.ShapeDtypeStruct
    return pl.pallas_call(
        functools.partial(signal_kernel, plan),
        out_shape=(
            shape((steps, SEGMENTS, channels), jnp.float32),
            shape((steps, SEGMENTS, channels), jnp.float32),
            shape((modes, SEGMENTS, channels), jnp.float32),
            shape((modes, channels), jnp.float32),
        ),
        in_specs=[SMEM] + [ANY] * (len(arrays) + 3) + [VMEM] * 4,
        out_specs=(VMEM,) * 4,
        scratch_shapes=[
            pltpu.VMEM((HALO + 2 * length, depth), jnp.bfloat16),
            pltpu.VMEM((2, depth, channels), jnp.bfloat16),
            pltpu.VMEM((channels // LANES, HALO + 2 * length, LANES), jnp.float32),
            pltpu.VMEM((channels // LANES, HALO + 2 * length, LANES), jnp.float32),
            pltpu.SemaphoreType.DMA((len(arrays), 4)),
        ],
        compiler_params=pltpu.CompilerParams(vmem_limit_bytes=48 * 1024 * 1024),
        name="signals",
    )(where, *arrays, mine, other, halo, taps, decay, amplitude, power)


def carry_kernel(
    where, signal, start_conv, before, carried, decay, amplitude, power, skip, keep, send, whole
):
    core = where[2]
    steps, _, channels = signal.shape
    length = keep.shape[0]
    modes = decay.shape[0]
    for low in range(0, channels, LANES):
        lanes = pl.ds(low, LANES)

        def spread(ref, *index):
            return jnp.broadcast_to(ref[(*index, lanes)].reshape(1, LANES), (SEGMENTS, LANES))

        direct = spread(skip, 0)
        decays = [spread(decay, mode) for mode in range(modes)]
        states = tuple(
            spread(amplitude, mode)
            * decays[mode]
            * (before[mode, :, lanes] + power[mode, :, lanes] * spread(carried, mode))
            for mode in range(modes)
        )

        def add(step, states):
            terms = list(states)
            while len(terms) > 1:
                terms = [terms[at] + terms[at + 1] for at in range(0, len(terms), 2)]
            total = start_conv[step, :, lanes] + terms[0] + direct * signal[step, :, lanes]
            whole[low // LANES, pl.ds(step, SEGMENTS, stride=steps), :] = total
            return tuple(decays[mode] * states[mode] for mode in range(modes))

        lax.fori_loop(0, steps, add, states, unroll=4)
    for group in range(channels // LANES):
        lanes = pl.ds(group * LANES, LANES)
        for out, block in ((keep, core), (send, 1 - core)):
            first = pl.multiple_of(block * length, SEGMENTS)
            out[:, lanes] = whole[group, pl.ds(first, length), :]


def carries(where, signal, start_conv, before, carried, decay, amplitude, power, skip):
    steps, _, channels = signal.shape
    length = steps * SEGMENTS // 2
    shape = jax.ShapeDtypeStruct
    return pl.pallas_call(
        carry_kernel,
        out_shape=(shape((length, channels), jnp.float32),) * 2,
        in_specs=[SMEM] + [VMEM] * 8,
        out_specs=(VMEM,) * 2,
        scratch_shapes=[pltpu.VMEM((channels // LANES, 2 * length, LANES), jnp.float32)],
        compiler_params=pltpu.CompilerParams(vmem_limit_bytes=32 * 1024 * 1024),
        name="carries",
    )(where, signal, start_conv, before, carried, decay, amplitude, power, skip)


def gate_kernel(where, tokens, halo, weight, taps, keep, taken, mixed, rows, weights, query, sems):
    core = where[2]
    length, depth = tokens.shape
    channels = weight.shape[1]
    parts = 4
    size = depth // parts
    copies = []
    for part in range(parts):
        span = pl.ds(part * size, size)
        group = (
            pltpu.make_async_copy(halo.at[:, span], rows.at[pl.ds(0, HALO), span], sems.at[part, 0]),
            pltpu.make_async_copy(
                tokens.at[:, span], rows.at[pl.ds(HALO, length), span], sems.at[part, 1]
            ),
            pltpu.make_async_copy(weight.at[span, :], weights.at[span, :], sems.at[part, 2]),
        )
        for copy in group:
            copy.start()
        copies.append(group)
    for part in range(parts):
        for copy in copies[part]:
            copy.wait()
        low, high = part * size, (part + 1) * size
        product = jnp.dot(
            rows[:, low:high], weights[low:high, :], preferred_element_type=jnp.float32
        )
        if part > 0:
            product = query[...] + product
        query[...] = rounded(product) if part == parts - 1 else product
    half = channels // 2
    block = 64
    for low in range(0, channels, LANES):
        lanes = pl.ds(low, LANES)
        inner = pl.ds(low % half, LANES)
        mine = core == low // half
        for row in range(0, length, block):
            total = taps[0, 0, lanes].reshape(1, LANES) * query[pl.ds(HALO + row, block), lanes]
            for offset in range(1, SHORT):
                total += (
                    taps[0, offset, lanes].reshape(1, LANES)
                    * query[pl.ds(HALO + row - offset, block), lanes]
                )
            span = pl.ds(row, block)
            conv = jnp.where(mine, keep[span, inner], taken[span, inner])
            mixed[span, lanes] = (total * conv).astype(jnp.bfloat16)


def gated(where, tokens, halo, weight, taps, keep, taken):
    length, depth = tokens.shape
    channels = weight.shape[1]
    return pl.pallas_call(
        gate_kernel,
        out_shape=jax.ShapeDtypeStruct((length, channels), jnp.bfloat16),
        in_specs=[SMEM, ANY, ANY, ANY, VMEM, VMEM, VMEM],
        out_specs=VMEM,
        scratch_shapes=[
            pltpu.VMEM((HALO + length, depth), jnp.bfloat16),
            pltpu.VMEM((depth, channels), jnp.bfloat16),
            pltpu.VMEM((HALO + length, channels), jnp.float32),
            pltpu.SemaphoreType.DMA((4, 3)),
        ],
        compiler_params=pltpu.CompilerParams(vmem_limit_bytes=32 * 1024 * 1024),
        name="gated",
    )(where, tokens, halo, weight, taps, keep, taken)


def carried_states(ends, rate, x, z, span):
    others = [along_z(ends, steps) for steps in range(1, Z)]
    carry = jnp.zeros_like(ends)
    line = ends * jnp.exp(-rate * (span * (Z - 1 - z)))
    for steps, state in zip(range(1, Z), others):
        source = (z - steps) % Z
        line = line + state * jnp.exp(-rate * (span * (Z - 1 - source)))
        carry = carry + jnp.where(z >= steps, state, 0.0) * jnp.exp(-rate * (span * (steps - 1)))
    others = [along_x(line, steps) for steps in range(1, X)]
    far = jnp.zeros_like(ends)
    for steps, state in zip(range(1, X), others):
        far = far + jnp.where(x >= steps, state, 0.0) * jnp.exp(-rate * (Z * span * (steps - 1)))
    return carry + far * jnp.exp(-rate * (span * z))


def local(tokens, in_weight, short_filter, residues, rates, skip):
    index = lax.axis_index("seq")
    core = index % CORES
    z = index // CORES % Z
    x = index // (CORES * Z)
    where = jnp.stack([x, z, core]).astype(jnp.int32)
    length = tokens.shape[0]
    channels = skip.shape[0]
    half = channels // 2
    span = CORES * length
    first = core == 0

    query_weight = lax.all_gather(in_weight[0], "seq", axis=0, tiled=True)

    low, high = in_weight[1:, :, :half], in_weight[1:, :, half:]
    own = jnp.where(first, low, high)
    received = swap_cores(jnp.where(first, high, low))
    block = jnp.concatenate(
        [jnp.where(first, own, received), jnp.where(first, received, own)], axis=1
    )
    pieces = gather_chips(block)

    other = swap_cores(tokens)
    tail, other_tail = tokens[length - HALO :], other[length - HALO :]
    halo = next_chip(jnp.where(first, other_tail, tail))
    query_halo = jnp.where(first, halo, other_tail)

    def half_of(array, axis):
        return lax.dynamic_slice_in_dim(array, core * half, half, axis)

    rate = half_of(rates, 0).T
    residue = half_of(residues, 0).T
    decay = jnp.exp(-rate)
    amplitude = residue * jnp.sqrt(-jnp.expm1(-2.0 * rate))
    step = span // SEGMENTS
    power = jnp.stack([jnp.exp(-rate * (step * distance)) for distance in (1, 2, 4)])
    starts = jnp.arange(SEGMENTS, dtype=jnp.float32)[None, :, None] * step
    start_power = jnp.exp(-rate[:, None, :] * starts)

    signal, start_conv, before, ends = signals(
        where, pieces, tokens, other, halo, half_of(short_filter, 2), decay, amplitude, power
    )
    carried = carried_states(ends, rate, x, z, span)
    keep, send = carries(
        where,
        signal,
        start_conv,
        before,
        carried,
        decay,
        amplitude,
        start_power,
        half_of(skip, 0)[None, :],
    )
    taken = swap_cores(send)
    return gated(where, tokens, query_halo, query_weight, short_filter, keep, taken)


def solution(mesh):
    placed = (
        P("seq", None),
        P(None, "seq", "mp"),
        P(None, None, "mp"),
        P("mp", None),
        P("mp", None),
        P("mp"),
    )
    return jax.shard_map(
        local, mesh=mesh, in_specs=placed, out_specs=P("seq", "mp"), check_vma=False
    )
```

```python
import functools
import math

import jax
import jax.numpy as jnp
from jax import lax
from jax.experimental import pallas as pl
from jax.experimental.pallas import tpu as pltpu
from jax.sharding import PartitionSpec as P

SHORT = 7
X, Z, CORES = 4, 4, 2
CHIPS = X * Z
HALO = 16
LANES = 128
SEGMENTS = 8

QUERY = pl.ds(0, 1)
KEY_VALUE = pl.ds(1, 2)

HBM = pl.BlockSpec(memory_space=pltpu.HBM)
VMEM = pl.BlockSpec(memory_space=pltpu.VMEM)
SMEM = pl.BlockSpec(memory_space=pltpu.SMEM)


def in_hbm(*arrays):
    return [pltpu.with_memory_space_constraint(array, pltpu.HBM) for array in arrays]


def in_vmem(*arrays):
    return [pltpu.with_memory_space_constraint(array, pltpu.VMEM) for array in arrays]


def place(x, z, core):
    return (x * Z + z) * CORES + core


def permute(value, target):
    pairs = []
    for x in range(X):
        for z in range(Z):
            for core in range(CORES):
                to = target(x, z, core)
                if to is not None:
                    pairs.append((place(x, z, core), place(*to)))
    return lax.ppermute(value, "seq", pairs)


def along_x(value, steps):
    return permute(value, lambda x, z, core: ((x + steps) % X, z, core))


def along_z(value, steps):
    return permute(value, lambda x, z, core: (x, (z + steps) % Z, core))


def swap_cores(value):
    return permute(value, lambda x, z, core: (x, z, 1 - core))


def next_chip(value, to_core):
    def target(x, z, core):
        chip = x * Z + z + 1
        if core != CORES - 1 or chip == CHIPS:
            return None
        return (chip // Z, chip % Z, to_core)

    return permute(value, target)


def together(*values):
    return lax.optimization_barrier(values)


def forwards(right, left):
    half = right.shape[1] // 2
    return along_x(right[:, :half], 1), along_x(left[:, half:], 3)


def sides(block):
    return along_x(block, 1), along_x(block, 3)


def with_sides(z_steps, block, right, left):
    height = block.shape[1]
    return [
        (x_steps, z_steps, 0, array, 0, height)
        for x_steps, array in ((0, block), (1, right), (3, left))
    ]


def with_far(z_steps, far_right, far_left):
    height = far_right.shape[1]
    return [(2, z_steps, 0, far_right, 0, height), (2, z_steps, height, far_left, 0, height)]


def rounded(value):
    return value.astype(jnp.bfloat16).astype(jnp.float32)


def start_copies(plan, streams, where, pieces, mine, other, halo, rows, weights, sems):
    x, z, core = where[0], where[1], where[2]
    length, depth = mine.shape
    groups = []
    offset = 0
    for at, (x_steps, z_steps, row, which, start, height) in enumerate(plan):
        chip = (x - x_steps + X) % X * Z + (z - z_steps + Z) % Z
        column = pl.multiple_of(chip * (depth // CHIPS) + row, LANES)
        copies = [
            pltpu.make_async_copy(
                pieces[which].at[streams, pl.ds(start, height), :],
                weights.at[:, pl.ds(offset, height), :],
                sems.at[at, 0],
            ),
            pltpu.make_async_copy(
                halo.at[:, pl.ds(column, height)],
                rows.at[pl.ds(0, HALO), pl.ds(offset, height)],
                sems.at[at, 1],
            ),
        ]
        for sem, array, block in ((2, mine, core), (3, other, 1 - core)):
            first = pl.multiple_of(HALO + block * length, HALO)
            copies.append(
                pltpu.make_async_copy(
                    array.at[:, pl.ds(column, height)],
                    rows.at[pl.ds(first, length), pl.ds(offset, height)],
                    sems.at[at, sem],
                )
            )
        for copy in copies:
            copy.start()
        groups.append((offset, height, copies))
        offset += height
    return groups


def multiply(groups, parts, rows, weights, before, totals, last):
    depth = rows.shape[1]
    streams, _, channels = weights.shape
    for part in range(parts):
        low, high = part * depth // parts, (part + 1) * depth // parts
        for offset, height, copies in groups:
            if low <= offset < high:
                for copy in copies:
                    copy.wait()
        for stream in range(streams):
            product = jnp.dot(
                rows[:, low:high], weights[stream, low:high, :], preferred_element_type=jnp.float32
            )
            source = before if part == 0 else totals
            for group in range(channels // LANES):
                share = product[:, group * LANES : (group + 1) * LANES]
                if source is not None:
                    share = source[stream, group] + share
                totals[stream, group] = rounded(share) if last and part == parts - 1 else share


def arrays_in(plan):
    return 1 + max(step[3] for step in plan)


def partial_kernel(plan, streams, parts, has_before, where, *refs):
    count = arrays_in(plan)
    pieces, refs = refs[:count], refs[count:]
    mine, other, halo = refs[:3]
    before, refs = (refs[3], refs[4:]) if has_before else (None, refs[3:])
    totals, rows, weights, sems = refs
    groups = start_copies(plan, streams, where, pieces, mine, other, halo, rows, weights, sems)
    multiply(groups, parts, rows, weights, before, totals, False)


def plan_of(pieces):
    arrays = []
    plan = []
    for x_steps, z_steps, row, array, start, height in pieces:
        which = next((at for at, seen in enumerate(arrays) if seen is array), len(arrays))
        if which == len(arrays):
            arrays.append(array)
        plan.append((x_steps, z_steps, row, which, start, height))
    return tuple(plan), arrays, sum(step[-1] for step in plan)


def copy_scratch(pieces, streams, mine):
    plan, arrays, depth = plan_of(pieces)
    channels = arrays[0].shape[2]
    return [
        pltpu.VMEM((HALO + 2 * mine.shape[0], depth), jnp.bfloat16),
        pltpu.VMEM((streams.size, depth, channels), jnp.bfloat16),
        pltpu.SemaphoreType.DMA((len(plan), 4)),
    ]


def partial_products(where, pieces, streams, mine, other, halo, before, parts, name):
    plan, arrays, _ = plan_of(pieces)
    channels = arrays[0].shape[2]
    more = [] if before is None else [before]
    shape = (streams.size, channels // LANES, HALO + 2 * mine.shape[0], LANES)
    return pl.pallas_call(
        functools.partial(partial_kernel, plan, streams, parts, before is not None),
        out_shape=pltpu.VMEM(shape, jnp.float32),
        in_specs=[SMEM] + [HBM] * (len(arrays) + 3) + [VMEM] * len(more),
        out_specs=VMEM,
        scratch_shapes=copy_scratch(pieces, streams, mine),
        compiler_params=pltpu.CompilerParams(vmem_limit_bytes=24 * 1024 * 1024),
        name=name,
    )(where, *in_hbm(*arrays, mine, other, halo), *in_vmem(*more))


def signal_kernel(plan, streams, where, *refs):
    count = arrays_in(plan)
    pieces, refs = refs[:count], refs[count:]
    mine, other, halo, products, taps, decay, amplitude, power = refs[:8]
    signal, start_conv, before, ends, rows, weights, sems, projected = refs[8:]
    channels = weights.shape[2]
    steps = 2 * mine.shape[0] // SEGMENTS
    groups = start_copies(plan, streams, where, pieces, mine, other, halo, rows, weights, sems)
    multiply(groups, 1, rows, weights, products, projected, True)
    for low in range(0, channels, LANES):
        lanes = pl.ds(low, LANES)
        group = low // LANES

        def spread(ref, *index):
            return jnp.broadcast_to(ref[(*index, lanes)].reshape(1, LANES), (SEGMENTS, LANES))

        def load(stream, step):
            return projected[stream, group, pl.ds(HALO + step, SEGMENTS, stride=steps), :]

        key_taps = [spread(taps, 1, offset) for offset in range(SHORT)]
        value_taps = [spread(taps, 2, offset) for offset in range(SHORT)]

        def featurize(step, carry):
            keys, values = carry
            keys = (load(0, step),) + keys
            values = (load(1, step),) + values
            total_key = key_taps[0] * keys[0]
            total_value = value_taps[0] * values[0]
            for offset in range(1, SHORT):
                total_key += key_taps[offset] * keys[offset]
                total_value += value_taps[offset] * values[offset]
            signal[step, :, lanes] = total_key * total_value
            return keys[:-1], values[:-1]

        lax.fori_loop(
            0,
            steps,
            featurize,
            (
                tuple(load(0, -offset) for offset in range(1, SHORT)),
                tuple(load(1, -offset) for offset in range(1, SHORT)),
            ),
            unroll=4,
        )
        modes = decay.shape[0]
        decays = [spread(decay, mode) for mode in range(modes)]
        amplitudes = [spread(amplitude, mode) for mode in range(modes)]

        def scan(step, states):
            here = signal[step, :, lanes]
            states = tuple(decays[mode] * states[mode] + here for mode in range(modes))
            terms = [amplitudes[mode] * states[mode] for mode in range(modes)]
            while len(terms) > 1:
                terms = [terms[at] + terms[at + 1] for at in range(0, len(terms), 2)]
            start_conv[step, :, lanes] = terms[0]
            return states

        empty = jnp.zeros((SEGMENTS, LANES), jnp.float32)
        states = lax.fori_loop(0, steps, scan, (empty,) * modes, unroll=2)
        segment = lax.broadcasted_iota(jnp.int32, (SEGMENTS, LANES), 0)
        for mode in range(modes):
            state = states[mode]
            for level, distance in enumerate((1, 2, 4)):
                moved = pltpu.roll(state, distance, 0)
                state = state + jnp.where(
                    segment >= distance, spread(power, level, mode) * moved, 0.0
                )
            before[mode, :, lanes] = jnp.where(segment >= 1, pltpu.roll(state, 1, 0), 0.0)
            ends[pl.ds(mode, 1), lanes] = state[SEGMENTS - 1 :, :]


def signals(where, pieces, mine, other, halo, products, taps, decay, amplitude, power):
    plan, arrays, _ = plan_of(pieces)
    modes, channels = decay.shape
    steps = 2 * mine.shape[0] // SEGMENTS
    return pl.pallas_call(
        functools.partial(signal_kernel, plan, KEY_VALUE),
        out_shape=(
            pltpu.VMEM((steps, SEGMENTS, channels), jnp.float32),
            pltpu.VMEM((steps, SEGMENTS, channels), jnp.float32),
            pltpu.VMEM((modes, SEGMENTS, channels), jnp.float32),
            jax.ShapeDtypeStruct((modes, channels), jnp.float32),
        ),
        in_specs=[SMEM] + [HBM] * (len(arrays) + 3) + [VMEM] * 5,
        out_specs=(VMEM,) * 4,
        scratch_shapes=copy_scratch(pieces, KEY_VALUE, mine) + [pltpu.VMEM(products.shape, jnp.float32)],
        compiler_params=pltpu.CompilerParams(vmem_limit_bytes=16 * 1024 * 1024),
        name="signals",
    )(
        where,
        *in_hbm(*arrays, mine, other, halo),
        *in_vmem(products),
        taps,
        decay,
        amplitude,
        power,
    )


def query_kernel(plan, streams, parts, where, *refs):
    count = arrays_in(plan)
    pieces, refs = refs[:count], refs[count:]
    mine, other, halo, taps, query, rows, weights, sems, projected = refs
    channels = weights.shape[2]
    steps = 2 * mine.shape[0] // SEGMENTS
    groups = start_copies(plan, streams, where, pieces, mine, other, halo, rows, weights, sems)
    multiply(groups, parts, rows, weights, None, projected, True)
    for group in range(channels // LANES):
        lanes = pl.ds(group * LANES, LANES)
        spread = [
            jnp.broadcast_to(taps[0, offset, lanes].reshape(1, LANES), (SEGMENTS, LANES))
            for offset in range(SHORT)
        ]

        def load(step):
            return projected[0, group, pl.ds(HALO + step, SEGMENTS, stride=steps), :]

        def featurize(step, held):
            held = (load(step),) + held
            total = spread[0] * held[0]
            for offset in range(1, SHORT):
                total += spread[offset] * held[offset]
            query[step, :, lanes] = total
            return held[:-1]

        held = tuple(load(-offset) for offset in range(1, SHORT))
        lax.fori_loop(0, steps, featurize, held, unroll=4)


def queries(where, pieces, mine, other, halo, taps):
    plan, arrays, _ = plan_of(pieces)
    channels = arrays[0].shape[2]
    rows = 2 * mine.shape[0]
    return pl.pallas_call(
        functools.partial(query_kernel, plan, QUERY, 4),
        out_shape=pltpu.VMEM((rows // SEGMENTS, SEGMENTS, channels), jnp.float32),
        in_specs=[SMEM] + [HBM] * (len(arrays) + 3) + [VMEM],
        out_specs=VMEM,
        scratch_shapes=copy_scratch(pieces, QUERY, mine)
        + [pltpu.VMEM((1, channels // LANES, HALO + rows, LANES), jnp.float32)],
        compiler_params=pltpu.CompilerParams(vmem_limit_bytes=24 * 1024 * 1024),
        name="queries",
    )(where, *in_hbm(*arrays, mine, other, halo), taps)


def gate_kernel(
    where,
    query,
    signal,
    start_conv,
    before,
    carried,
    decay,
    amplitude,
    power,
    skip,
    keep,
    send,
    whole,
):
    core = where[2]
    steps, _, channels = signal.shape
    length = keep.shape[0]
    modes = decay.shape[0]
    for low in range(0, channels, LANES):
        lanes = pl.ds(low, LANES)

        def spread(ref, *index):
            return jnp.broadcast_to(ref[(*index, lanes)].reshape(1, LANES), (SEGMENTS, LANES))

        direct = spread(skip, 0)
        decays = [spread(decay, mode) for mode in range(modes)]
        states = tuple(
            spread(amplitude, mode)
            * decays[mode]
            * (before[mode, :, lanes] + power[mode, :, lanes] * spread(carried, mode))
            for mode in range(modes)
        )

        def add(step, states):
            terms = list(states)
            while len(terms) > 1:
                terms = [terms[at] + terms[at + 1] for at in range(0, len(terms), 2)]
            total = start_conv[step, :, lanes] + terms[0] + direct * signal[step, :, lanes]
            whole[low // LANES, pl.ds(step, SEGMENTS, stride=steps), :] = (
                query[step, :, lanes] * total
            )
            return tuple(decays[mode] * states[mode] for mode in range(modes))

        lax.fori_loop(0, steps, add, states, unroll=4)
    for group in range(channels // LANES):
        lanes = pl.ds(group * LANES, LANES)
        for out, block in ((keep, core), (send, 1 - core)):
            first = pl.multiple_of(block * length, SEGMENTS)
            out[:, lanes] = whole[group, pl.ds(first, length), :].astype(jnp.bfloat16)


def gated(where, query, signal, start_conv, before, carried, decay, amplitude, power, skip):
    steps, _, channels = signal.shape
    length = steps * SEGMENTS // 2
    return pl.pallas_call(
        gate_kernel,
        out_shape=(jax.ShapeDtypeStruct((length, channels), jnp.bfloat16),) * 2,
        in_specs=[SMEM] + [VMEM] * 9,
        out_specs=(VMEM,) * 2,
        scratch_shapes=[pltpu.VMEM((channels // LANES, 2 * length, LANES), jnp.float32)],
        compiler_params=pltpu.CompilerParams(vmem_limit_bytes=16 * 1024 * 1024),
        name="gated",
    )(
        where,
        *in_vmem(query, signal, start_conv, before),
        carried,
        decay,
        amplitude,
        power,
        skip,
    )


def carried_states(ends, rate, x, z, span):
    others = [along_z(ends, steps) for steps in range(1, Z)]
    carry = jnp.zeros_like(ends)
    line = ends * jnp.exp(-rate * (span * (Z - 1 - z)))
    for steps, state in zip(range(1, Z), others):
        source = (z - steps) % Z
        line = line + state * jnp.exp(-rate * (span * (Z - 1 - source)))
        carry = carry + jnp.where(z >= steps, state, 0.0) * jnp.exp(-rate * (span * (steps - 1)))
    others = [along_x(line, steps) for steps in range(1, X)]
    far = jnp.zeros_like(ends)
    for steps, state in zip(range(1, X), others):
        far = far + jnp.where(x >= steps, state, 0.0) * jnp.exp(-rate * (Z * span * (steps - 1)))
    return carry + far * jnp.exp(-rate * (span * z))


def local(tokens, in_weight, short_filter, residues, rates, skip):
    index = lax.axis_index("seq")
    core = index % CORES
    z = index // CORES % Z
    x = index // (CORES * Z)
    where = jnp.stack([x, z, core]).astype(jnp.int32)
    length = tokens.shape[0]
    channels = skip.shape[0]
    half = channels // 2
    span = CORES * length
    first = core == 0

    def half_of(array, axis):
        return lax.dynamic_slice_in_dim(array, core * half, half, axis)

    low, high = in_weight[:, :, :half], in_weight[:, :, half:]
    own = jnp.where(first, low, high)
    received = swap_cores(jnp.where(first, high, low))
    block = jnp.concatenate(
        [jnp.where(first, own, received), jnp.where(first, received, own)], axis=1
    )
    up, down = along_z(block, 1), along_z(block, 3)
    right, left = sides(block)
    other = swap_cores(tokens)
    tail = tokens[length - HALO :]
    halo, other_halo = next_chip(tail, 0), next_chip(tail, 1)
    up, right, left, held, other, halo, other_halo = together(
        up, right, left, block, other, halo, other_halo
    )
    halo = halo + other_halo
    near = with_sides(0, block, right, left)

    across = along_z(held, 2)
    far = forwards(right, left)
    right, left = sides(up)
    right, left, far_right, far_left, down = together(right, left, *far, down)
    near += with_far(0, far_right, far_left) + with_sides(1, up, right, left)

    far = forwards(right, left)
    right, left = sides(down)
    right, left, far_right, far_left, across = together(right, left, *far, across)
    near += with_far(1, far_right, far_left) + with_sides(3, down, right, left)
    pieces = near

    far = forwards(right, left)
    right, left = sides(across)
    products = partial_products(where, near, KEY_VALUE, tokens, other, halo, None, 2, "early")
    right, left, far_right, far_left, products = together(right, left, *far, products)
    near = with_far(3, far_right, far_left) + with_sides(2, across, right, left)

    last = with_far(2, *forwards(right, left))

    rate = half_of(rates, 0).T
    residue = half_of(residues, 0).T
    decay = jnp.exp(-rate)
    amplitude = residue * jnp.sqrt(-jnp.expm1(-2.0 * rate))
    step = span // SEGMENTS
    power = jnp.stack([jnp.exp(-rate * (step * distance)) for distance in (1, 2, 4)])
    starts = jnp.arange(SEGMENTS, dtype=jnp.float32)[None, :, None] * step
    start_power = jnp.exp(-rate[:, None, :] * starts)
    taps = half_of(short_filter, 2)

    products = partial_products(where, near, KEY_VALUE, tokens, other, halo, products, 1, "near")
    signal, start_conv, before, ends = signals(
        where, last, tokens, other, halo, products, taps, decay, amplitude, power
    )
    query = queries(where, pieces + near + last, tokens, other, halo, taps)
    carried = carried_states(ends, rate, x, z, span)
    keep, send = gated(
        where,
        query,
        signal,
        start_conv,
        before,
        carried,
        decay,
        amplitude,
        start_power,
        half_of(skip, 0)[None, :],
    )
    taken = swap_cores(send)
    return jnp.concatenate(
        [jnp.where(first, keep, taken), jnp.where(first, taken, keep)], axis=1
    )


def solution(mesh):
    placed = (
        P("seq", None),
        P(None, "seq", "mp"),
        P(None, None, "mp"),
        P("mp", None),
        P("mp", None),
        P("mp"),
    )
    return jax.shard_map(
        local, mesh=mesh, in_specs=placed, out_specs=P("seq", "mp"), check_vma=False
    )
```

```python
import functools
import math

import jax
import jax.numpy as jnp
from jax import lax
from jax.experimental import pallas as pl
from jax.experimental.pallas import tpu as pltpu
from jax.sharding import PartitionSpec as P

SHORT = 7
X, Z, CORES = 4, 4, 2
CHIPS = X * Z
HALO = 16
LANES = 128
SEGMENTS = 8
BEFORE = 8

QUERY = pl.ds(0, 1)
KEY_VALUE = pl.ds(1, 2)
ALL = pl.ds(0, 3)

ANY = pl.BlockSpec(memory_space=pl.ANY)
HBM = pl.BlockSpec(memory_space=pltpu.HBM)
VMEM = pl.BlockSpec(memory_space=pltpu.VMEM)
SMEM = pl.BlockSpec(memory_space=pltpu.SMEM)


def in_hbm(*arrays):
    return [pltpu.with_memory_space_constraint(array, pltpu.HBM) for array in arrays]


def in_vmem(*arrays):
    return [pltpu.with_memory_space_constraint(array, pltpu.VMEM) for array in arrays]


def place(x, z, core):
    return (x * Z + z) * CORES + core


def permute(value, target):
    pairs = []
    for x in range(X):
        for z in range(Z):
            for core in range(CORES):
                to = target(x, z, core)
                if to is not None:
                    pairs.append((place(x, z, core), place(*to)))
    return lax.ppermute(value, "seq", pairs)


def along_x(value, steps):
    return permute(value, lambda x, z, core: ((x + steps) % X, z, core))


def along_z(value, steps):
    return permute(value, lambda x, z, core: (x, (z + steps) % Z, core))


def across_z(value, mask):
    return permute(value, lambda x, z, core: (x, z ^ mask, core))


def swap_cores(value):
    return permute(value, lambda x, z, core: (x, z, 1 - core))


def next_chip(value):
    def target(x, z, core):
        chip = x * Z + z + 1
        return (chip // Z, chip % Z, core) if chip < CHIPS else None

    return permute(value, target)


def together(*values):
    return lax.optimization_barrier(values)


def halves_kernel(right, left, right_half, left_half, sems):
    half = right_half.shape[1]
    copies = [
        pltpu.make_async_copy(right.at[:, pl.ds(0, half), :], right_half, sems.at[0]),
        pltpu.make_async_copy(left.at[:, pl.ds(half, half), :], left_half, sems.at[1]),
    ]
    for copy in copies:
        copy.start()
    for copy in copies:
        copy.wait()


def forwards(right, left):
    streams, height, channels = right.shape
    half = pltpu.VMEM((streams, height // 2, channels), right.dtype)
    right, left = pl.pallas_call(
        halves_kernel,
        out_shape=(half, half),
        in_specs=[ANY] * 2,
        out_specs=(VMEM,) * 2,
        scratch_shapes=[pltpu.SemaphoreType.DMA((2,))],
        compiler_params=pltpu.CompilerParams(vmem_limit_bytes=2 * 1024 * 1024),
        name="halves",
    )(right, left)
    return along_x(right, 1), along_x(left, 3)


def sides(block):
    return along_x(block, 1), along_x(block, 3)


def with_sides(z_mask, block, right, left):
    height = block.shape[1]
    return [
        (x_steps, z_mask, 0, array, 0, height)
        for x_steps, array in ((0, block), (1, right), (3, left))
    ]


def with_far(z_mask, far_right, far_left):
    height = far_right.shape[1]
    return [(2, z_mask, 0, far_right, 0, height), (2, z_mask, height, far_left, 0, height)]


def rounded(value):
    return value.astype(jnp.bfloat16).astype(jnp.float32)


def start_copies(plan, streams, where, pieces, mine, other, halo, rows, weights, sems):
    x, z, core = where[0], where[1], where[2]
    parts = []
    if halo is not None:
        parts.append((1, halo, 0))
    if mine is not None:
        base = HALO if halo is not None else 0
        length = mine.shape[0]
        parts += [(2, mine, base + core * length), (3, other, base + (1 - core) * length)]
    depth = CHIPS * 2 * LANES
    copies = []
    offset = 0
    for at, (x_steps, z_mask, row, which, start, height) in enumerate(plan):
        chip = (x - x_steps + X) % X * Z + (z ^ z_mask)
        column = pl.multiple_of(chip * (depth // CHIPS) + row, LANES)
        copies.append(
            pltpu.make_async_copy(
                pieces[which].at[streams, pl.ds(start, height), :],
                weights.at[:, pl.ds(offset, height), :],
                sems.at[at, 0],
            )
        )
        for sem, array, first in parts:
            if array is not halo:
                first = pl.multiple_of(first, HALO)
            copies.append(
                pltpu.make_async_copy(
                    array.at[:, pl.ds(column, height)],
                    rows.at[pl.ds(first, array.shape[0]), pl.ds(offset, height)],
                    sems.at[at, sem],
                )
            )
        offset += height
    for copy in copies:
        copy.start()
    return copies


def multiply(copies, rows, weights, finish):
    for copy in copies:
        copy.wait()
    streams, _, channels = weights.shape
    for stream in range(streams):
        product = jnp.dot(rows[...], weights[stream], preferred_element_type=jnp.float32)
        for group in range(channels // LANES):
            finish(stream, group, product[:, group * LANES : (group + 1) * LANES])


def segmented(ref, before, halo_before, first_stream):
    stride = ref.shape[2] // SEGMENTS
    steps = stride - BEFORE

    def finish(stream, group, share):
        main = rounded(before[first_stream + stream, group] + share[HALO:])
        head = rounded(halo_before[first_stream + stream, group] + share[:HALO])
        ref[stream, group, 0:BEFORE, :] = head[HALO - BEFORE :]
        ref[stream, group, BEFORE:stride, :] = main[:steps]
        for segment in range(1, SEGMENTS):
            first = segment * steps - BEFORE
            ref[stream, group, segment * stride : (segment + 1) * stride, :] = main[
                first : first + stride
            ]

    def load(stream, group, step):
        return ref[stream, group, pl.ds(BEFORE + step, SEGMENTS, stride=stride), :]

    return finish, load


def segment_scratch(streams, rows, channels):
    return pltpu.VMEM((streams.size, channels // LANES, rows + SEGMENTS * BEFORE, LANES), jnp.float32)


def arrays_in(plan):
    return 1 + max(step[3] for step in plan)


def partial_kernel(plan, has_main, has_halo, has_before, where, *refs):
    count = arrays_in(plan)
    pieces, refs = refs[:count], list(refs[count:])
    mine, other = (refs.pop(0), refs.pop(0)) if has_main else (None, None)
    halo = refs.pop(0) if has_halo else None
    before = refs.pop(0) if has_main and has_before else None
    halo_before = refs.pop(0) if has_halo and has_before else None
    totals = refs.pop(0) if has_main else None
    halo_totals = refs.pop(0) if has_halo else None
    rows, weights, sems = refs
    copies = start_copies(plan, ALL, where, pieces, mine, other, halo, rows, weights, sems)

    def finish(stream, group, share):
        if has_halo:
            head = share[:HALO]
            halo_totals[stream, group] = (
                head if halo_before is None else halo_before[stream, group] + head
            )
            share = share[HALO:]
        if has_main:
            totals[stream, group] = share if before is None else before[stream, group] + share

    multiply(copies, rows, weights, finish)


def plan_of(pieces):
    arrays = []
    plan = []
    for x_steps, z_mask, row, array, start, height in pieces:
        which = next((at for at, seen in enumerate(arrays) if seen is array), len(arrays))
        if which == len(arrays):
            arrays.append(array)
        plan.append((x_steps, z_mask, row, which, start, height))
    return tuple(plan), arrays, sum(step[-1] for step in plan)


def copy_scratch(pieces, streams, rows):
    plan, arrays, depth = plan_of(pieces)
    channels = arrays[0].shape[2]
    return [
        pltpu.VMEM((rows, depth), jnp.bfloat16),
        pltpu.VMEM((streams.size, depth, channels), jnp.bfloat16),
        pltpu.SemaphoreType.DMA((len(plan), 4)),
    ]


def partial_products(where, pieces, tokens, halo, before, name):
    plan, arrays, _ = plan_of(pieces)
    channels = arrays[0].shape[2]
    heights = [sum(array.shape[0] for array in tokens)] if tokens else []
    heights += [HALO] if halo else []
    shapes = [
        pltpu.VMEM((ALL.size, channels // LANES, height, LANES), jnp.float32) for height in heights
    ]
    inputs = [*arrays, *tokens, *halo]
    return pl.pallas_call(
        functools.partial(partial_kernel, plan, bool(tokens), bool(halo), bool(before)),
        out_shape=shapes,
        in_specs=[SMEM] + [HBM] * len(inputs) + [VMEM] * len(before),
        out_specs=[VMEM] * len(shapes),
        scratch_shapes=copy_scratch(pieces, ALL, sum(heights)),
        compiler_params=pltpu.CompilerParams(vmem_limit_bytes=8 * 1024 * 1024),
        name=name,
    )(where, *in_hbm(*inputs), *in_vmem(*before))


def signal_kernel(plan, streams, where, *refs):
    count = arrays_in(plan)
    pieces, refs = refs[:count], refs[count:]
    mine, other, halo, products, halo_products = refs[:5]
    taps, decay, amplitude, power, skip = refs[5:10]
    signal, before, ends, rows, weights, sems, projected = refs[10:]
    channels = weights.shape[2]
    steps = 2 * mine.shape[0] // SEGMENTS
    copies = start_copies(plan, streams, where, pieces, mine, other, halo, rows, weights, sems)
    finish, load = segmented(projected, products, halo_products, streams.start)
    multiply(copies, rows, weights, finish)
    for low in range(0, channels, LANES):
        lanes = pl.ds(low, LANES)
        group = low // LANES

        def spread(ref, *index):
            return jnp.broadcast_to(ref[(*index, lanes)].reshape(1, LANES), (SEGMENTS, LANES))

        key_taps = [spread(taps, 1, offset) for offset in range(SHORT)]
        value_taps = [spread(taps, 2, offset) for offset in range(SHORT)]

        def featurize(step, carry):
            keys, values = carry
            keys = (load(0, group, step),) + keys
            values = (load(1, group, step),) + values
            total_key = key_taps[0] * keys[0]
            total_value = value_taps[0] * values[0]
            for offset in range(1, SHORT):
                total_key += key_taps[offset] * keys[offset]
                total_value += value_taps[offset] * values[offset]
            signal[step, :, lanes] = total_key * total_value
            return keys[:-1], values[:-1]

        lax.fori_loop(
            0,
            steps,
            featurize,
            (
                tuple(load(0, group, -offset) for offset in range(1, SHORT)),
                tuple(load(1, group, -offset) for offset in range(1, SHORT)),
            ),
            unroll=8,
        )
        modes = decay.shape[0]
        decays = [spread(decay, mode) for mode in range(modes)]
        amplitudes = [spread(amplitude, mode) for mode in range(modes)]
        direct = spread(skip, 0)

        def scan(step, states):
            here = signal[step, :, lanes]
            states = tuple(decays[mode] * states[mode] + here for mode in range(modes))
            terms = [amplitudes[mode] * states[mode] for mode in range(modes)]
            while len(terms) > 1:
                terms = [terms[at] + terms[at + 1] for at in range(0, len(terms), 2)]
            signal[step, :, lanes] = terms[0] + direct * here
            return states

        empty = jnp.zeros((SEGMENTS, LANES), jnp.float32)
        states = lax.fori_loop(0, steps, scan, (empty,) * modes, unroll=8)
        segment = lax.broadcasted_iota(jnp.int32, (SEGMENTS, LANES), 0)
        for mode in range(modes):
            state = states[mode]
            for level, distance in enumerate((1, 2, 4)):
                moved = pltpu.roll(state, distance, 0)
                state = state + jnp.where(
                    segment >= distance, spread(power, level, mode) * moved, 0.0
                )
            before[mode, :, lanes] = jnp.where(segment >= 1, pltpu.roll(state, 1, 0), 0.0)
            ends[pl.ds(mode, 1), lanes] = state[SEGMENTS - 1 :, :]


def signals(where, pieces, tokens, halo, products, taps, decay, amplitude, power, skip):
    plan, arrays, _ = plan_of(pieces)
    modes, channels = decay.shape
    rows = sum(array.shape[0] for array in tokens)
    inputs = [*arrays, *tokens, halo]
    return pl.pallas_call(
        functools.partial(signal_kernel, plan, KEY_VALUE),
        out_shape=(
            pltpu.VMEM((rows // SEGMENTS, SEGMENTS, channels), jnp.float32),
            pltpu.VMEM((modes, SEGMENTS, channels), jnp.float32),
            jax.ShapeDtypeStruct((modes, channels), jnp.float32),
        ),
        in_specs=[SMEM] + [HBM] * len(inputs) + [VMEM] * 7,
        out_specs=(VMEM,) * 3,
        scratch_shapes=copy_scratch(pieces, KEY_VALUE, HALO + rows)
        + [segment_scratch(KEY_VALUE, rows, channels)],
        compiler_params=pltpu.CompilerParams(vmem_limit_bytes=8 * 1024 * 1024),
        name="signals",
    )(where, *in_hbm(*inputs), *in_vmem(*products), taps, decay, amplitude, power, skip)


def query_kernel(plan, streams, where, *refs):
    count = arrays_in(plan)
    pieces, refs = refs[:count], refs[count:]
    mine, other, halo, products, halo_products, conv, taps = refs[:7]
    query, gated, rows, weights, sems, projected = refs[7:]
    channels = weights.shape[2]
    steps = 2 * mine.shape[0] // SEGMENTS
    copies = start_copies(plan, streams, where, pieces, mine, other, halo, rows, weights, sems)
    finish, load = segmented(projected, products, halo_products, streams.start)
    multiply(copies, rows, weights, finish)
    for group in range(channels // LANES):
        lanes = pl.ds(group * LANES, LANES)
        spread = [
            jnp.broadcast_to(taps[0, offset, lanes].reshape(1, LANES), (SEGMENTS, LANES))
            for offset in range(SHORT)
        ]

        def featurize(step, held):
            held = (load(0, group, step),) + held
            total = spread[0] * held[0]
            for offset in range(1, SHORT):
                total += spread[offset] * held[offset]
            query[step, :, lanes] = total
            gated[step, :, lanes] = total * conv[step, :, lanes]
            return held[:-1]

        held = tuple(load(0, group, -offset) for offset in range(1, SHORT))
        lax.fori_loop(0, steps, featurize, held, unroll=8)


def queries(where, pieces, tokens, halo, products, conv, taps):
    plan, arrays, _ = plan_of(pieces)
    channels = arrays[0].shape[2]
    rows = sum(array.shape[0] for array in tokens)
    inputs = [*arrays, *tokens, halo]
    return pl.pallas_call(
        functools.partial(query_kernel, plan, QUERY),
        out_shape=(pltpu.VMEM((rows // SEGMENTS, SEGMENTS, channels), jnp.float32),) * 2,
        in_specs=[SMEM] + [HBM] * len(inputs) + [VMEM] * 4,
        out_specs=(VMEM,) * 2,
        scratch_shapes=copy_scratch(pieces, QUERY, HALO + rows)
        + [segment_scratch(QUERY, rows, channels)],
        compiler_params=pltpu.CompilerParams(vmem_limit_bytes=8 * 1024 * 1024),
        name="queries",
    )(where, *in_hbm(*inputs), *in_vmem(*products, conv), taps)


def gate_kernel(
    where,
    query,
    gated,
    before,
    carried,
    decay,
    amplitude,
    power,
    keep,
    send,
    whole,
):
    core = where[2]
    steps, _, channels = query.shape
    length = keep.shape[0]
    modes = decay.shape[0]
    for low in range(0, channels, LANES):
        lanes = pl.ds(low, LANES)

        def spread(ref, *index):
            return jnp.broadcast_to(ref[(*index, lanes)].reshape(1, LANES), (SEGMENTS, LANES))

        decays = [spread(decay, mode) for mode in range(modes)]
        states = tuple(
            spread(amplitude, mode)
            * decays[mode]
            * (before[mode, :, lanes] + power[mode, :, lanes] * spread(carried, mode))
            for mode in range(modes)
        )

        def add(step, states):
            terms = list(states)
            while len(terms) > 1:
                terms = [terms[at] + terms[at + 1] for at in range(0, len(terms), 2)]
            whole[0, low // LANES, pl.ds(step, SEGMENTS, stride=steps + BEFORE), :] = (
                gated[step, :, lanes] + query[step, :, lanes] * terms[0]
            )
            return tuple(decays[mode] * states[mode] for mode in range(modes))

        lax.fori_loop(0, steps, add, states, unroll=8)
    for group in range(channels // LANES):
        lanes = pl.ds(group * LANES, LANES)
        for out, block in ((keep, core), (send, 1 - core)):
            for segment in range(SEGMENTS // CORES):
                first = (block * (SEGMENTS // CORES) + segment) * (steps + BEFORE)
                first = pl.multiple_of(first, SEGMENTS)
                out[pl.ds(segment * steps, steps), lanes] = whole[
                    0, group, pl.ds(first, steps), :
                ].astype(jnp.bfloat16)


def carry_gated(where, query, gated, before, carried, decay, amplitude, power):
    steps, _, channels = query.shape
    length = steps * SEGMENTS // 2
    return pl.pallas_call(
        gate_kernel,
        out_shape=(jax.ShapeDtypeStruct((length, channels), jnp.bfloat16),) * 2,
        in_specs=[SMEM] + [VMEM] * 7,
        out_specs=(VMEM,) * 2,
        scratch_shapes=[segment_scratch(QUERY, 2 * length, channels)],
        compiler_params=pltpu.CompilerParams(vmem_limit_bytes=8 * 1024 * 1024),
        name="gated",
    )(where, *in_vmem(query, gated, before), carried, decay, amplitude, power)


def carry_factors(rate, x, z, span):
    x, z = x.astype(jnp.float32), z.astype(jnp.float32)

    def after(tokens):
        return jnp.exp(-rate * tokens)

    def if_before(position, steps):
        return jnp.where(position >= steps, 1.0, 0.0)

    line = [after(span * (Z - 1 - z))]
    for steps in range(1, Z):
        source = jnp.where(z >= steps, z - steps, z - steps + Z)
        line.append(after(span * (Z - 1 - source)))
    near = [if_before(z, steps) * after(float(span * (steps - 1))) for steps in range(1, Z)]
    far = [
        if_before(x, steps) * after(span * (Z * (steps - 1) + z)) for steps in range(1, X)
    ]
    return jnp.stack(line + near + far)


def carried_states(ends, factors):
    line, near, far = factors[:Z], factors[Z : 2 * Z - 1], factors[2 * Z - 1 :]
    others = [along_z(ends, steps) for steps in range(1, Z)]
    total, carry = line[0] * ends, 0.0
    for at, state in enumerate(others):
        total = total + line[at + 1] * state
        carry = carry + near[at] * state
    for at, state in enumerate([along_x(total, steps) for steps in range(1, X)]):
        carry = carry + far[at] * state
    return carry


def local(tokens, in_weight, short_filter, residues, rates, skip):
    index = lax.axis_index("seq")
    core = index % CORES
    z = index // CORES % Z
    x = index // (CORES * Z)
    where = jnp.stack([x, z, core]).astype(jnp.int32)
    length = tokens.shape[0]
    channels = skip.shape[0]
    half = channels // 2
    span = CORES * length
    first = core == 0

    def half_of(array, axis):
        return lax.dynamic_slice_in_dim(array, core * half, half, axis)

    low, high = in_weight[:, :, :half], in_weight[:, :, half:]
    own = jnp.where(first, low, high)
    received = swap_cores(jnp.where(first, high, low))
    tail = tokens[length - HALO :]
    tail = jnp.where(first, swap_cores(tail), tail)
    block = jnp.concatenate(
        [jnp.where(first, own, received), jnp.where(first, received, own)], axis=1
    )
    rate = half_of(rates, 0).T
    residue = half_of(residues, 0).T
    decay = jnp.exp(-rate)
    amplitude = residue * jnp.sqrt(-jnp.expm1(-2.0 * rate))
    step = span // SEGMENTS
    power = jnp.stack([jnp.exp(-rate * (step * distance)) for distance in (1, 2, 4)])
    starts = jnp.arange(SEGMENTS, dtype=jnp.float32)[None, :, None] * step
    start_power = jnp.exp(-rate[:, None, :] * starts)
    factors = carry_factors(rate, x, z, span)
    taps = half_of(short_filter, 2)
    direct = half_of(skip, 0)[None, :]

    beside = across_z(block, 1)
    right, left = sides(block)
    other = swap_cores(tokens)
    halo = next_chip(tail)
    held, other = together(block, other)
    over = across_z(held, 2)
    beside, right, left, held = together(beside, right, left, held)
    both = (tokens, other)

    far = forwards(right, left)
    pieces = with_sides(0, block, right, left)
    products = partial_products(where, pieces, both, (), (), "first")
    right, left = sides(beside)
    right, left, *far, over, products, halo = together(right, left, *far, over, *products, halo)
    so_far = pieces

    pieces = with_sides(1, beside, right, left) + with_far(0, *far)
    products = partial_products(where, pieces, both, (), (products,), "second")
    so_far += pieces
    halo_products = partial_products(where, so_far, (), (halo,), (), "halo")
    far = forwards(right, left)
    opposite = across_z(over, 1)
    right, left = sides(over)
    right, left, far_right, far_left, opposite, products, halo_products = together(
        right, left, *far, opposite, *products, *halo_products
    )

    pieces = with_sides(2, over, right, left) + with_far(1, far_right, far_left)
    products = partial_products(where, pieces, both, (halo,), (products, halo_products), "third")
    far = forwards(right, left)
    right, left = sides(opposite)
    small = (power, start_power, factors, decay, amplitude, taps, direct)
    right, left, far_right, far_left, products, halo_products, *small = together(
        right, left, *far, *products, *small
    )
    power, start_power, factors, decay, amplitude, taps, direct = small

    pieces = with_sides(3, opposite, right, left) + with_far(2, far_right, far_left)
    last = with_far(3, *forwards(right, left))
    products = partial_products(where, pieces, both, (halo,), (products, halo_products), "fourth")

    conv, before, ends = signals(
        where, last, both, halo, products, taps, decay, amplitude, power, direct
    )
    query, product = queries(where, last, both, halo, products, conv, taps)
    carried = carried_states(ends, factors)
    keep, send = carry_gated(
        where, query, product, before, carried, decay, amplitude, start_power
    )
    taken = swap_cores(send)
    return jnp.concatenate(
        [jnp.where(first, keep, taken), jnp.where(first, taken, keep)], axis=1
    )


def solution(mesh):
    placed = (
        P("seq", None),
        P(None, "seq", "mp"),
        P(None, None, "mp"),
        P("mp", None),
        P("mp", None),
        P("mp"),
    )
    return jax.shard_map(
        local, mesh=mesh, in_specs=placed, out_specs=P("seq", "mp"), check_vma=False
    )
```

```python
import functools
import math

import jax
import jax.numpy as jnp
from jax import lax
from jax.experimental import pallas as pl
from jax.experimental.pallas import tpu as pltpu
from jax.sharding import PartitionSpec as P

SHORT = 7
X, Z, CORES = 4, 4, 2
CHIPS = X * Z
HALO = 16
LANES = 128
SEGMENTS = 8
BEFORE = 8

QUERY = pl.ds(0, 1)
KEY_VALUE = pl.ds(1, 2)
ALL = pl.ds(0, 3)

ANY = pl.BlockSpec(memory_space=pl.ANY)
HBM = pl.BlockSpec(memory_space=pltpu.HBM)
VMEM = pl.BlockSpec(memory_space=pltpu.VMEM)
SMEM = pl.BlockSpec(memory_space=pltpu.SMEM)


def in_hbm(*arrays):
    return [pltpu.with_memory_space_constraint(array, pltpu.HBM) for array in arrays]


def in_vmem(*arrays):
    return [pltpu.with_memory_space_constraint(array, pltpu.VMEM) for array in arrays]


def place(x, z, core):
    return (x * Z + z) * CORES + core


def permute(value, target):
    pairs = []
    for x in range(X):
        for z in range(Z):
            for core in range(CORES):
                to = target(x, z, core)
                if to is not None:
                    pairs.append((place(x, z, core), place(*to)))
    return lax.ppermute(value, "seq", pairs)


def along_x(value, steps):
    return permute(value, lambda x, z, core: ((x + steps) % X, z, core))


def along_z(value, steps):
    return permute(value, lambda x, z, core: (x, (z + steps) % Z, core))


def across_z(value, mask):
    return permute(value, lambda x, z, core: (x, z ^ mask, core))


def swap_cores(value):
    return permute(value, lambda x, z, core: (x, z, 1 - core))


def next_chip(value):
    def target(x, z, core):
        chip = x * Z + z + 1
        return (chip // Z, chip % Z, core) if chip < CHIPS else None

    return permute(value, target)


def together(*values):
    return lax.optimization_barrier(values)


def halves_kernel(right, left, right_half, left_half, sems):
    half = right_half.shape[1]
    copies = [
        pltpu.make_async_copy(right.at[:, pl.ds(0, half), :], right_half, sems.at[0]),
        pltpu.make_async_copy(left.at[:, pl.ds(half, half), :], left_half, sems.at[1]),
    ]
    for copy in copies:
        copy.start()
    for copy in copies:
        copy.wait()


def forwards(right, left):
    streams, height, channels = right.shape
    half = pltpu.VMEM((streams, height // 2, channels), right.dtype)
    right, left = pl.pallas_call(
        halves_kernel,
        out_shape=(half, half),
        in_specs=[ANY] * 2,
        out_specs=(VMEM,) * 2,
        scratch_shapes=[pltpu.SemaphoreType.DMA((2,))],
        compiler_params=pltpu.CompilerParams(vmem_limit_bytes=2 * 1024 * 1024),
        name="halves",
    )(right, left)
    return along_x(right, 1), along_x(left, 3)


def sides(block):
    return along_x(block, 1), along_x(block, 3)


def with_sides(z_mask, block, right, left):
    height = block.shape[1]
    return [
        (x_steps, z_mask, 0, array, 0, height)
        for x_steps, array in ((0, block), (1, right), (3, left))
    ]


def with_far(z_mask, far_right, far_left):
    height = far_right.shape[1]
    return [(2, z_mask, 0, far_right, 0, height), (2, z_mask, height, far_left, 0, height)]


def rounded(value):
    return value.astype(jnp.bfloat16).astype(jnp.float32)


def start_copies(plan, streams, where, pieces, mine, other, halo, rows, weights, sems):
    x, z, core = where[0], where[1], where[2]
    parts = []
    if halo is not None:
        parts.append((1, halo, 0))
    if mine is not None:
        base = HALO if halo is not None else 0
        length = mine.shape[0]
        parts += [(2, mine, base + core * length), (3, other, base + (1 - core) * length)]
    depth = CHIPS * 2 * LANES
    copies = []
    offset = 0
    for at, (x_steps, z_mask, row, which, start, height) in enumerate(plan):
        chip = (x - x_steps + X) % X * Z + (z ^ z_mask)
        column = pl.multiple_of(chip * (depth // CHIPS) + row, LANES)
        copies.append(
            pltpu.make_async_copy(
                pieces[which].at[streams, pl.ds(start, height), :],
                weights.at[:, pl.ds(offset, height), :],
                sems.at[at, 0],
            )
        )
        for sem, array, first in parts:
            if array is not halo:
                first = pl.multiple_of(first, HALO)
            copies.append(
                pltpu.make_async_copy(
                    array.at[:, pl.ds(column, height)],
                    rows.at[pl.ds(first, array.shape[0]), pl.ds(offset, height)],
                    sems.at[at, sem],
                )
            )
        offset += height
    for copy in copies:
        copy.start()
    return copies


def columns_to(rows, where, x_steps, z_mask, mine, other, halo, sems):
    x, z, core = where[0], where[1], where[2]
    length, width = mine.shape[0], rows.shape[1]
    chip = (x - x_steps + X) % X * Z + (z ^ z_mask)
    span = pl.ds(pl.multiple_of(chip * width, LANES), width)
    copies = [pltpu.make_async_copy(halo.at[:, span], rows.at[pl.ds(0, HALO), :], sems.at[0])]
    for sem, array, block in ((1, mine, core), (2, other, 1 - core)):
        first = pl.multiple_of(HALO + block * length, HALO)
        copies.append(
            pltpu.make_async_copy(
                array.at[:, span], rows.at[pl.ds(first, length), :], sems.at[sem]
            )
        )
    for copy in copies:
        copy.start()
    return copies


def multiply(rows, weights, finish):
    for stream, weight in enumerate(weights):
        channels = weight.shape[1]
        product = jnp.dot(rows[...], weight, preferred_element_type=jnp.float32)
        for group in range(channels // LANES):
            finish(stream, group, product[:, group * LANES : (group + 1) * LANES])


def segmented(ref, before, halo_before, first_stream):
    stride = ref.shape[2] // SEGMENTS
    steps = stride - BEFORE

    def finish(stream, group, share):
        main = rounded(before[first_stream + stream, group] + share[HALO:])
        head = rounded(halo_before[first_stream + stream, group] + share[:HALO])
        ref[stream, group, 0:BEFORE, :] = head[HALO - BEFORE :]
        ref[stream, group, BEFORE:stride, :] = main[:steps]
        for segment in range(1, SEGMENTS):
            first = segment * steps - BEFORE
            ref[stream, group, segment * stride : (segment + 1) * stride, :] = main[
                first : first + stride
            ]

    def load(stream, group, step):
        return ref[stream, group, pl.ds(BEFORE + step, SEGMENTS, stride=stride), :]

    return finish, load


def segment_scratch(streams, rows, channels):
    return pltpu.VMEM((streams.size, channels // LANES, rows + SEGMENTS * BEFORE, LANES), jnp.float32)


def arrays_in(plan):
    return 1 + max(step[3] for step in plan)


def partial_kernel(plan, has_main, has_halo, has_before, kept_from, where, *refs):
    count = arrays_in(plan)
    pieces, refs = refs[:count], list(refs[count:])
    mine, other = (refs.pop(0), refs.pop(0)) if has_main else (None, None)
    halo = refs.pop(0) if has_halo else None
    before = refs.pop(0) if has_main and has_before else None
    halo_before = refs.pop(0) if has_halo and has_before else None
    totals = refs.pop(0) if has_main else None
    halo_totals = refs.pop(0) if has_halo else None
    kept = refs.pop(0) if kept_from else None
    rows, weights, sems, kept_sems = refs
    copies = start_copies(plan, ALL, where, pieces, mine, other, halo, rows, weights, sems)
    kept_copies = (
        columns_to(kept, where, *kept_from, mine, other, halo, kept_sems) if kept_from else []
    )

    def finish(stream, group, share):
        if has_halo:
            head = share[:HALO]
            halo_totals[stream, group] = (
                head if halo_before is None else halo_before[stream, group] + head
            )
            share = share[HALO:]
        if has_main:
            totals[stream, group] = share if before is None else before[stream, group] + share

    for copy in copies:
        copy.wait()
    multiply(rows, [weights[stream] for stream in range(ALL.size)], finish)
    for copy in kept_copies:
        copy.wait()


def plan_of(pieces):
    arrays = []
    plan = []
    for x_steps, z_mask, row, array, start, height in pieces:
        which = next((at for at, seen in enumerate(arrays) if seen is array), len(arrays))
        if which == len(arrays):
            arrays.append(array)
        plan.append((x_steps, z_mask, row, which, start, height))
    return tuple(plan), arrays, sum(step[-1] for step in plan)


def copy_scratch(pieces, streams, rows):
    plan, arrays, depth = plan_of(pieces)
    channels = arrays[0].shape[2]
    return [
        pltpu.VMEM((rows, depth), jnp.bfloat16),
        pltpu.VMEM((streams.size, depth, channels), jnp.bfloat16),
        pltpu.SemaphoreType.DMA((len(plan), 4)),
        pltpu.SemaphoreType.DMA((3,)),
    ]


def partial_products(where, pieces, tokens, halo, before, name, kept_from=None):
    plan, arrays, _ = plan_of(pieces)
    channels = arrays[0].shape[2]
    heights = [sum(array.shape[0] for array in tokens)] if tokens else []
    heights += [HALO] if halo else []
    shapes = [
        pltpu.VMEM((ALL.size, channels // LANES, height, LANES), jnp.float32) for height in heights
    ]
    if kept_from:
        shapes.append(pltpu.VMEM((sum(heights), 2 * LANES), jnp.bfloat16))
    inputs = [*arrays, *tokens, *halo]
    return pl.pallas_call(
        functools.partial(
            partial_kernel, plan, bool(tokens), bool(halo), bool(before), kept_from
        ),
        out_shape=shapes,
        in_specs=[SMEM] + [HBM] * len(inputs) + [VMEM] * len(before),
        out_specs=[VMEM] * len(shapes),
        scratch_shapes=copy_scratch(pieces, ALL, sum(heights)),
        compiler_params=pltpu.CompilerParams(vmem_limit_bytes=8 * 1024 * 1024),
        name=name,
    )(where, *in_hbm(*inputs), *in_vmem(*before))


def last_weights(upper, lower, streams):
    return [
        jnp.concatenate([upper[stream], lower[stream]], axis=0)
        for stream in range(streams.start, streams.start + streams.size)
    ]


def signal_kernel(
    rows,
    upper,
    lower,
    products,
    halo_products,
    taps,
    decay,
    amplitude,
    power,
    skip,
    signal,
    before,
    ends,
    projected,
):
    channels = upper.shape[2]
    steps = signal.shape[0]
    finish, load = segmented(projected, products, halo_products, KEY_VALUE.start)
    multiply(rows, last_weights(upper, lower, KEY_VALUE), finish)
    for low in range(0, channels, LANES):
        lanes = pl.ds(low, LANES)
        group = low // LANES

        def spread(ref, *index):
            return jnp.broadcast_to(ref[(*index, lanes)].reshape(1, LANES), (SEGMENTS, LANES))

        key_taps = [spread(taps, 1, offset) for offset in range(SHORT)]
        value_taps = [spread(taps, 2, offset) for offset in range(SHORT)]

        def featurize(step, carry):
            keys, values = carry
            keys = (load(0, group, step),) + keys
            values = (load(1, group, step),) + values
            total_key = key_taps[0] * keys[0]
            total_value = value_taps[0] * values[0]
            for offset in range(1, SHORT):
                total_key += key_taps[offset] * keys[offset]
                total_value += value_taps[offset] * values[offset]
            signal[step, :, lanes] = total_key * total_value
            return keys[:-1], values[:-1]

        lax.fori_loop(
            0,
            steps,
            featurize,
            (
                tuple(load(0, group, -offset) for offset in range(1, SHORT)),
                tuple(load(1, group, -offset) for offset in range(1, SHORT)),
            ),
            unroll=8,
        )
        modes = decay.shape[0]
        decays = [spread(decay, mode) for mode in range(modes)]
        amplitudes = [spread(amplitude, mode) for mode in range(modes)]
        direct = spread(skip, 0)

        def scan(step, states):
            here = signal[step, :, lanes]
            states = tuple(decays[mode] * states[mode] + here for mode in range(modes))
            terms = [amplitudes[mode] * states[mode] for mode in range(modes)]
            while len(terms) > 1:
                terms = [terms[at] + terms[at + 1] for at in range(0, len(terms), 2)]
            signal[step, :, lanes] = terms[0] + direct * here
            return states

        empty = jnp.zeros((SEGMENTS, LANES), jnp.float32)
        states = lax.fori_loop(0, steps, scan, (empty,) * modes, unroll=8)
        segment = lax.broadcasted_iota(jnp.int32, (SEGMENTS, LANES), 0)
        for mode in range(modes):
            state = states[mode]
            for level, distance in enumerate((1, 2, 4)):
                moved = pltpu.roll(state, distance, 0)
                state = state + jnp.where(
                    segment >= distance, spread(power, level, mode) * moved, 0.0
                )
            before[mode, :, lanes] = jnp.where(segment >= 1, pltpu.roll(state, 1, 0), 0.0)
            ends[pl.ds(mode, 1), lanes] = state[SEGMENTS - 1 :, :]


def signals(rows, last, products, taps, decay, amplitude, power, skip):
    modes, channels = decay.shape
    length = rows.shape[0] - HALO
    return pl.pallas_call(
        signal_kernel,
        out_shape=(
            pltpu.VMEM((length // SEGMENTS, SEGMENTS, channels), jnp.float32),
            pltpu.VMEM((modes, SEGMENTS, channels), jnp.float32),
            jax.ShapeDtypeStruct((modes, channels), jnp.float32),
        ),
        in_specs=[VMEM] * 10,
        out_specs=(VMEM,) * 3,
        scratch_shapes=[segment_scratch(KEY_VALUE, length, channels)],
        compiler_params=pltpu.CompilerParams(vmem_limit_bytes=8 * 1024 * 1024),
        name="signals",
    )(*in_vmem(rows, *last, *products), taps, decay, amplitude, power, skip)


def query_kernel(
    rows, upper, lower, products, halo_products, conv, taps, query, gated, projected
):
    channels = upper.shape[2]
    steps = conv.shape[0]
    finish, load = segmented(projected, products, halo_products, QUERY.start)
    multiply(rows, last_weights(upper, lower, QUERY), finish)
    for group in range(channels // LANES):
        lanes = pl.ds(group * LANES, LANES)
        spread = [
            jnp.broadcast_to(taps[0, offset, lanes].reshape(1, LANES), (SEGMENTS, LANES))
            for offset in range(SHORT)
        ]

        def featurize(step, held):
            held = (load(0, group, step),) + held
            total = spread[0] * held[0]
            for offset in range(1, SHORT):
                total += spread[offset] * held[offset]
            query[step, :, lanes] = total
            gated[step, :, lanes] = total * conv[step, :, lanes]
            return held[:-1]

        held = tuple(load(0, group, -offset) for offset in range(1, SHORT))
        lax.fori_loop(0, steps, featurize, held, unroll=8)


def queries(rows, last, products, conv, taps):
    steps, _, channels = conv.shape
    return pl.pallas_call(
        query_kernel,
        out_shape=(pltpu.VMEM(conv.shape, jnp.float32),) * 2,
        in_specs=[VMEM] * 7,
        out_specs=(VMEM,) * 2,
        scratch_shapes=[segment_scratch(QUERY, steps * SEGMENTS, channels)],
        compiler_params=pltpu.CompilerParams(vmem_limit_bytes=8 * 1024 * 1024),
        name="queries",
    )(*in_vmem(rows, *last, *products, conv), taps)


def gate_kernel(
    where,
    query,
    gated,
    before,
    carried,
    decay,
    amplitude,
    power,
    keep,
    send,
    whole,
):
    core = where[2]
    steps, _, channels = query.shape
    length = keep.shape[0]
    modes = decay.shape[0]
    for low in range(0, channels, LANES):
        lanes = pl.ds(low, LANES)

        def spread(ref, *index):
            return jnp.broadcast_to(ref[(*index, lanes)].reshape(1, LANES), (SEGMENTS, LANES))

        decays = [spread(decay, mode) for mode in range(modes)]
        states = tuple(
            spread(amplitude, mode)
            * decays[mode]
            * (before[mode, :, lanes] + power[mode, :, lanes] * spread(carried, mode))
            for mode in range(modes)
        )

        def add(step, states):
            terms = list(states)
            while len(terms) > 1:
                terms = [terms[at] + terms[at + 1] for at in range(0, len(terms), 2)]
            whole[0, low // LANES, pl.ds(step, SEGMENTS, stride=steps + BEFORE), :] = (
                gated[step, :, lanes] + query[step, :, lanes] * terms[0]
            )
            return tuple(decays[mode] * states[mode] for mode in range(modes))

        lax.fori_loop(0, steps, add, states, unroll=8)
    for group in range(channels // LANES):
        lanes = pl.ds(group * LANES, LANES)
        for out, block in ((keep, core), (send, 1 - core)):
            for segment in range(SEGMENTS // CORES):
                first = (block * (SEGMENTS // CORES) + segment) * (steps + BEFORE)
                first = pl.multiple_of(first, SEGMENTS)
                out[pl.ds(segment * steps, steps), lanes] = whole[
                    0, group, pl.ds(first, steps), :
                ].astype(jnp.bfloat16)


def carry_gated(where, query, gated, before, carried, decay, amplitude, power):
    steps, _, channels = query.shape
    length = steps * SEGMENTS // 2
    return pl.pallas_call(
        gate_kernel,
        out_shape=(jax.ShapeDtypeStruct((length, channels), jnp.bfloat16),) * 2,
        in_specs=[SMEM] + [VMEM] * 7,
        out_specs=(VMEM,) * 2,
        scratch_shapes=[segment_scratch(QUERY, 2 * length, channels)],
        compiler_params=pltpu.CompilerParams(vmem_limit_bytes=8 * 1024 * 1024),
        name="gated",
    )(where, *in_vmem(query, gated, before), carried, decay, amplitude, power)


def carry_factors(rate, x, z, span):
    x, z = x.astype(jnp.float32), z.astype(jnp.float32)

    def after(tokens):
        return jnp.exp(-rate * tokens)

    def if_before(position, steps):
        return jnp.where(position >= steps, 1.0, 0.0)

    line = [after(span * (Z - 1 - z))]
    for steps in range(1, Z):
        source = jnp.where(z >= steps, z - steps, z - steps + Z)
        line.append(after(span * (Z - 1 - source)))
    near = [if_before(z, steps) * after(float(span * (steps - 1))) for steps in range(1, Z)]
    far = [
        if_before(x, steps) * after(span * (Z * (steps - 1) + z)) for steps in range(1, X)
    ]
    return jnp.stack(line + near + far)


def carried_states(ends, factors):
    line, near, far = factors[:Z], factors[Z : 2 * Z - 1], factors[2 * Z - 1 :]
    others = [along_z(ends, steps) for steps in range(1, Z)]
    total, carry = line[0] * ends, 0.0
    for at, state in enumerate(others):
        total = total + line[at + 1] * state
        carry = carry + near[at] * state
    for at, state in enumerate([along_x(total, steps) for steps in range(1, X)]):
        carry = carry + far[at] * state
    return carry


def local(tokens, in_weight, short_filter, residues, rates, skip):
    index = lax.axis_index("seq")
    core = index % CORES
    z = index // CORES % Z
    x = index // (CORES * Z)
    where = jnp.stack([x, z, core]).astype(jnp.int32)
    length = tokens.shape[0]
    channels = skip.shape[0]
    half = channels // 2
    span = CORES * length
    first = core == 0

    def half_of(array, axis):
        return lax.dynamic_slice_in_dim(array, core * half, half, axis)

    low, high = in_weight[:, :, :half], in_weight[:, :, half:]
    own = jnp.where(first, low, high)
    received, later_tokens = together(swap_cores(jnp.where(first, high, low)), tokens)
    block = jnp.concatenate(
        [jnp.where(first, own, received), jnp.where(first, received, own)], axis=1
    )
    beside = across_z(block, 1)
    right, left = sides(block)
    other = swap_cores(later_tokens)
    held, tail = together(block, later_tokens[length - HALO :])
    held, other_tail = together(held, swap_cores(tail))
    over = across_z(held, 2)
    halo = next_chip(jnp.where(first, other_tail, tail))
    beside, right, left, other, *parameters = together(
        beside, right, left, other, rates, residues, short_filter, skip
    )
    rates, residues, short_filter, skip = parameters
    both = (tokens, other)

    rate = half_of(rates, 0).T
    residue = half_of(residues, 0).T
    decay = jnp.exp(-rate)
    amplitude = residue * jnp.sqrt(-jnp.expm1(-2.0 * rate))
    step = span // SEGMENTS
    power = jnp.stack([jnp.exp(-rate * (step * distance)) for distance in (1, 2, 4)])
    starts = jnp.arange(SEGMENTS, dtype=jnp.float32)[None, :, None] * step
    start_power = jnp.exp(-rate[:, None, :] * starts)
    factors = carry_factors(rate, x, z, span)
    taps = half_of(short_filter, 2)
    direct = half_of(skip, 0)[None, :]

    far = forwards(right, left)
    pieces = with_sides(0, block, right, left)
    products = partial_products(where, pieces, both, (), (), "first")
    right, left = sides(beside)
    far_beside = forwards(right, left)
    right, left, *far, over, products, halo, far_right, far_left = together(
        right, left, *far, over, *products, halo, *far_beside
    )
    so_far = pieces

    opposite = across_z(over, 1)
    pieces = with_sides(1, beside, right, left) + with_far(0, *far)
    products = partial_products(where, pieces, both, (), (products,), "second")
    so_far += pieces
    right, left = sides(over)
    right, left, opposite, products = together(right, left, opposite, *products)

    pieces = with_sides(2, over, right, left) + with_far(1, far_right, far_left)
    products = partial_products(where, pieces, both, (), (products,), "third")
    so_far += pieces
    halo_products = partial_products(where, so_far, (), (halo,), (), "halo")
    far = forwards(right, left)
    right, left = sides(opposite)
    small = (power, start_power, factors, decay, amplitude, taps, direct)
    right, left, far_right, far_left, products, halo_products, *small = together(
        right, left, *far, *products, *halo_products, *small
    )
    power, start_power, factors, decay, amplitude, taps, direct = small

    pieces = with_sides(3, opposite, right, left) + with_far(2, far_right, far_left)
    last = forwards(right, left)
    *products, rows = partial_products(
        where, pieces, both, (halo,), (products, halo_products), "fourth", (2, 3)
    )

    conv, before, ends = signals(
        rows, last, products, taps, decay, amplitude, power, direct
    )
    query, product = queries(rows, last, products, conv, taps)
    carried = carried_states(ends, factors)
    keep, send = carry_gated(
        where, query, product, before, carried, decay, amplitude, start_power
    )
    taken = swap_cores(send)
    return jnp.concatenate(
        [jnp.where(first, keep, taken), jnp.where(first, taken, keep)], axis=1
    )


def solution(mesh):
    placed = (
        P("seq", None),
        P(None, "seq", "mp"),
        P(None, None, "mp"),
        P("mp", None),
        P("mp", None),
        P("mp"),
    )
    return jax.shard_map(
        local, mesh=mesh, in_specs=placed, out_specs=P("seq", "mp"), check_vma=False
    )
```

```python
import functools
import math

import jax
import jax.numpy as jnp
from jax import lax
from jax.experimental import pallas as pl
from jax.experimental.pallas import tpu as pltpu
from jax.sharding import PartitionSpec as P

SHORT = 7
X, Z, CORES = 4, 4, 2
CHIPS = X * Z
HALO = 16
LANES = 128
SEGMENTS = 8
BEFORE = 8

QUERY = pl.ds(0, 1)
KEY_VALUE = pl.ds(1, 2)
ALL = pl.ds(0, 3)

ANY = pl.BlockSpec(memory_space=pl.ANY)
HBM = pl.BlockSpec(memory_space=pltpu.HBM)
VMEM = pl.BlockSpec(memory_space=pltpu.VMEM)
SMEM = pl.BlockSpec(memory_space=pltpu.SMEM)


def in_hbm(*arrays):
    return [pltpu.with_memory_space_constraint(array, pltpu.HBM) for array in arrays]


def in_vmem(*arrays):
    return [pltpu.with_memory_space_constraint(array, pltpu.VMEM) for array in arrays]


def place(x, z, core):
    return (x * Z + z) * CORES + core


def permute(value, target):
    pairs = []
    for x in range(X):
        for z in range(Z):
            for core in range(CORES):
                to = target(x, z, core)
                if to is not None:
                    pairs.append((place(x, z, core), place(*to)))
    return lax.ppermute(value, "seq", pairs)


def along_x(value, steps):
    return permute(value, lambda x, z, core: ((x + steps) % X, z, core))


def along_z(value, steps):
    return permute(value, lambda x, z, core: (x, (z + steps) % Z, core))


def across_z(value, mask):
    return permute(value, lambda x, z, core: (x, z ^ mask, core))


def swap_cores(value):
    return permute(value, lambda x, z, core: (x, z, 1 - core))


def next_chip(value):
    def target(x, z, core):
        chip = x * Z + z + 1
        return (chip // Z, chip % Z, core) if chip < CHIPS else None

    return permute(value, target)


def together(*values):
    return lax.optimization_barrier(values)


def halves_kernel(right, left, right_half, left_half, sems):
    half = right_half.shape[1]
    copies = [
        pltpu.make_async_copy(right.at[:, pl.ds(0, half), :], right_half, sems.at[0]),
        pltpu.make_async_copy(left.at[:, pl.ds(half, half), :], left_half, sems.at[1]),
    ]
    for copy in copies:
        copy.start()
    for copy in copies:
        copy.wait()


def forwards(right, left):
    streams, height, channels = right.shape
    half = pltpu.VMEM((streams, height // 2, channels), right.dtype)
    right, left = pl.pallas_call(
        halves_kernel,
        out_shape=(half, half),
        in_specs=[ANY] * 2,
        out_specs=(VMEM,) * 2,
        scratch_shapes=[pltpu.SemaphoreType.DMA((2,))],
        compiler_params=pltpu.CompilerParams(vmem_limit_bytes=2 * 1024 * 1024),
        name="halves",
    )(right, left)
    return along_x(right, 1), along_x(left, 3)


def sides(block):
    return along_x(block, 1), along_x(block, 3)


def with_sides(z_mask, block, *both_sides):
    height = block.shape[1]
    return [
        (x_steps, z_mask, 0, array, 0, height)
        for x_steps, array in zip((0, 1, 3), (block, *both_sides))
    ]


def with_far(z_mask, far_right, far_left):
    height = far_right.shape[1]
    return [(2, z_mask, 0, far_right, 0, height), (2, z_mask, height, far_left, 0, height)]


def rounded(value):
    return value.astype(jnp.bfloat16).astype(jnp.float32)


def start_copies(plan, streams, where, pieces, mine, other, halo, rows, weights, sems):
    x, z, core = where[0], where[1], where[2]
    parts = []
    if halo is not None:
        parts.append((1, halo, 0))
    if mine is not None:
        base = HALO if halo is not None else 0
        length = mine.shape[0]
        parts += [(2, mine, base + core * length), (3, other, base + (1 - core) * length)]
    depth = CHIPS * 2 * LANES
    copies = []
    offset = 0
    for at, (x_steps, z_mask, row, which, start, height) in enumerate(plan):
        chip = (x - x_steps + X) % X * Z + (z ^ z_mask)
        column = pl.multiple_of(chip * (depth // CHIPS) + row, LANES)
        copies.append(
            pltpu.make_async_copy(
                pieces[which].at[streams, pl.ds(start, height), :],
                weights.at[:, pl.ds(offset, height), :],
                sems.at[at, 0],
            )
        )
        for sem, array, first in parts:
            if array is not halo:
                first = pl.multiple_of(first, HALO)
            copies.append(
                pltpu.make_async_copy(
                    array.at[:, pl.ds(column, height)],
                    rows.at[pl.ds(first, array.shape[0]), pl.ds(offset, height)],
                    sems.at[at, sem],
                )
            )
        offset += height
    for copy in copies:
        copy.start()
    return copies


def columns_to(rows, where, chips, mine, other, halo, sems):
    x, z, core = where[0], where[1], where[2]
    length, width = mine.shape[0], 2 * LANES
    copies = []
    for at, (x_steps, z_mask) in enumerate(chips):
        chip = (x - x_steps + X) % X * Z + (z ^ z_mask)
        span = pl.ds(pl.multiple_of(chip * width, LANES), width)
        into = pl.ds(at * width, width)
        for sem, array, first in (
            (0, halo, 0),
            (1, mine, HALO + core * length),
            (2, other, HALO + (1 - core) * length),
        ):
            first = first if sem == 0 else pl.multiple_of(first, HALO)
            copies.append(
                pltpu.make_async_copy(
                    array.at[:, span],
                    rows.at[pl.ds(first, array.shape[0]), into],
                    sems.at[at, sem],
                )
            )
    for copy in copies:
        copy.start()
    return copies


def multiply(rows, weights, finish):
    for stream, weight in enumerate(weights):
        channels = weight.shape[1]
        product = jnp.dot(rows[...], weight, preferred_element_type=jnp.float32)
        for group in range(channels // LANES):
            finish(stream, group, product[:, group * LANES : (group + 1) * LANES])


def segmented(ref, before, halo_before, first_stream):
    stride = ref.shape[2] // SEGMENTS
    steps = stride - BEFORE

    def finish(stream, group, share):
        main = rounded(before[first_stream + stream, group] + share[HALO:])
        head = rounded(halo_before[first_stream + stream, group] + share[:HALO])
        ref[stream, group, 0:BEFORE, :] = head[HALO - BEFORE :]
        ref[stream, group, BEFORE:stride, :] = main[:steps]
        for segment in range(1, SEGMENTS):
            first = segment * steps - BEFORE
            ref[stream, group, segment * stride : (segment + 1) * stride, :] = main[
                first : first + stride
            ]

    def load(stream, group, step):
        return ref[stream, group, pl.ds(BEFORE + step, SEGMENTS, stride=stride), :]

    return finish, load


def segment_scratch(streams, rows, channels):
    return pltpu.VMEM((streams.size, channels // LANES, rows + SEGMENTS * BEFORE, LANES), jnp.float32)


def arrays_in(plan):
    return 1 + max(step[3] for step in plan)


def partial_kernel(plan, has_main, has_halo, has_before, kept_from, where, *refs):
    count = arrays_in(plan)
    pieces, refs = refs[:count], list(refs[count:])
    mine, other = (refs.pop(0), refs.pop(0)) if has_main else (None, None)
    halo = refs.pop(0) if has_halo else None
    before = refs.pop(0) if has_main and has_before else None
    halo_before = refs.pop(0) if has_halo and has_before else None
    totals = refs.pop(0) if has_main else None
    halo_totals = refs.pop(0) if has_halo else None
    kept = refs.pop(0) if kept_from else None
    rows, weights, sems, kept_sems = refs
    copies = start_copies(plan, ALL, where, pieces, mine, other, halo, rows, weights, sems)
    kept_copies = (
        columns_to(kept, where, kept_from, mine, other, halo, kept_sems) if kept_from else []
    )

    def finish(stream, group, share):
        if has_halo:
            head = share[:HALO]
            halo_totals[stream, group] = (
                head if halo_before is None else halo_before[stream, group] + head
            )
            share = share[HALO:]
        if has_main:
            totals[stream, group] = share if before is None else before[stream, group] + share

    for copy in copies:
        copy.wait()
    multiply(rows, [weights[stream] for stream in range(ALL.size)], finish)
    for copy in kept_copies:
        copy.wait()


def plan_of(pieces):
    arrays = []
    plan = []
    for x_steps, z_mask, row, array, start, height in pieces:
        which = next((at for at, seen in enumerate(arrays) if seen is array), len(arrays))
        if which == len(arrays):
            arrays.append(array)
        plan.append((x_steps, z_mask, row, which, start, height))
    return tuple(plan), arrays, sum(step[-1] for step in plan)


def copy_scratch(pieces, streams, rows):
    plan, arrays, depth = plan_of(pieces)
    channels = arrays[0].shape[2]
    return [
        pltpu.VMEM((rows, depth), jnp.bfloat16),
        pltpu.VMEM((streams.size, depth, channels), jnp.bfloat16),
        pltpu.SemaphoreType.DMA((len(plan), 4)),
        pltpu.SemaphoreType.DMA((3, 3)),
    ]


def partial_products(where, pieces, tokens, halo, before, name, kept_from=None):
    plan, arrays, _ = plan_of(pieces)
    channels = arrays[0].shape[2]
    heights = [sum(array.shape[0] for array in tokens)] if tokens else []
    heights += [HALO] if halo else []
    shapes = [
        pltpu.VMEM((ALL.size, channels // LANES, height, LANES), jnp.float32) for height in heights
    ]
    if kept_from:
        shapes.append(pltpu.VMEM((sum(heights), len(kept_from) * 2 * LANES), jnp.bfloat16))
    inputs = [*arrays, *tokens, *halo]
    return pl.pallas_call(
        functools.partial(
            partial_kernel, plan, bool(tokens), bool(halo), bool(before), kept_from
        ),
        out_shape=shapes,
        in_specs=[SMEM] + [HBM] * len(inputs) + [VMEM] * len(before),
        out_specs=[VMEM] * len(shapes),
        scratch_shapes=copy_scratch(pieces, ALL, sum(heights)),
        compiler_params=pltpu.CompilerParams(vmem_limit_bytes=8 * 1024 * 1024),
        name=name,
    )(where, *in_hbm(*inputs), *in_vmem(*before))


def last_weights(last, streams):
    return [
        jnp.concatenate([array[stream] for array in last], axis=0)
        for stream in range(streams.start, streams.start + streams.size)
    ]


def signal_kernel(count, rows, *refs):
    last, refs = refs[:count], refs[count:]
    products, halo_products, taps, decay, amplitude, power, skip = refs[:7]
    signal, before, ends, projected = refs[7:]
    channels = last[0].shape[2]
    steps = signal.shape[0]
    finish, load = segmented(projected, products, halo_products, KEY_VALUE.start)
    multiply(rows, last_weights(last, KEY_VALUE), finish)
    for low in range(0, channels, LANES):
        lanes = pl.ds(low, LANES)
        group = low // LANES

        def spread(ref, *index):
            return jnp.broadcast_to(ref[(*index, lanes)].reshape(1, LANES), (SEGMENTS, LANES))

        key_taps = [spread(taps, 1, offset) for offset in range(SHORT)]
        value_taps = [spread(taps, 2, offset) for offset in range(SHORT)]

        def featurize(step, carry):
            keys, values = carry
            keys = (load(0, group, step),) + keys
            values = (load(1, group, step),) + values
            total_key = key_taps[0] * keys[0]
            total_value = value_taps[0] * values[0]
            for offset in range(1, SHORT):
                total_key += key_taps[offset] * keys[offset]
                total_value += value_taps[offset] * values[offset]
            signal[step, :, lanes] = total_key * total_value
            return keys[:-1], values[:-1]

        lax.fori_loop(
            0,
            steps,
            featurize,
            (
                tuple(load(0, group, -offset) for offset in range(1, SHORT)),
                tuple(load(1, group, -offset) for offset in range(1, SHORT)),
            ),
            unroll=8,
        )
        modes = decay.shape[0]
        decays = [spread(decay, mode) for mode in range(modes)]
        amplitudes = [spread(amplitude, mode) for mode in range(modes)]
        direct = spread(skip, 0)

        def scan(step, states):
            here = signal[step, :, lanes]
            states = tuple(decays[mode] * states[mode] + here for mode in range(modes))
            terms = [amplitudes[mode] * states[mode] for mode in range(modes)]
            while len(terms) > 1:
                terms = [terms[at] + terms[at + 1] for at in range(0, len(terms), 2)]
            signal[step, :, lanes] = terms[0] + direct * here
            return states

        empty = jnp.zeros((SEGMENTS, LANES), jnp.float32)
        states = lax.fori_loop(0, steps, scan, (empty,) * modes, unroll=8)
        segment = lax.broadcasted_iota(jnp.int32, (SEGMENTS, LANES), 0)
        for mode in range(modes):
            state = states[mode]
            for level, distance in enumerate((1, 2, 4)):
                moved = pltpu.roll(state, distance, 0)
                state = state + jnp.where(
                    segment >= distance, spread(power, level, mode) * moved, 0.0
                )
            before[mode, :, lanes] = jnp.where(segment >= 1, pltpu.roll(state, 1, 0), 0.0)
            ends[pl.ds(mode, 1), lanes] = state[SEGMENTS - 1 :, :]


def signals(rows, last, products, taps, decay, amplitude, power, skip):
    modes, channels = decay.shape
    length = rows.shape[0] - HALO
    return pl.pallas_call(
        functools.partial(signal_kernel, len(last)),
        out_shape=(
            pltpu.VMEM((length // SEGMENTS, SEGMENTS, channels), jnp.float32),
            pltpu.VMEM((modes, SEGMENTS, channels), jnp.float32),
            jax.ShapeDtypeStruct((modes, channels), jnp.float32),
        ),
        in_specs=[VMEM] * (len(last) + 8),
        out_specs=(VMEM,) * 3,
        scratch_shapes=[segment_scratch(KEY_VALUE, length, channels)],
        compiler_params=pltpu.CompilerParams(vmem_limit_bytes=8 * 1024 * 1024),
        name="signals",
    )(*in_vmem(rows, *last, *products), taps, decay, amplitude, power, skip)


def query_kernel(count, rows, *refs):
    last, refs = refs[:count], refs[count:]
    products, halo_products, conv, taps, query, gated, projected = refs
    channels = last[0].shape[2]
    steps = conv.shape[0]
    finish, load = segmented(projected, products, halo_products, QUERY.start)
    multiply(rows, last_weights(last, QUERY), finish)
    for group in range(channels // LANES):
        lanes = pl.ds(group * LANES, LANES)
        spread = [
            jnp.broadcast_to(taps[0, offset, lanes].reshape(1, LANES), (SEGMENTS, LANES))
            for offset in range(SHORT)
        ]

        def featurize(step, held):
            held = (load(0, group, step),) + held
            total = spread[0] * held[0]
            for offset in range(1, SHORT):
                total += spread[offset] * held[offset]
            query[step, :, lanes] = total
            gated[step, :, lanes] = total * conv[step, :, lanes]
            return held[:-1]

        held = tuple(load(0, group, -offset) for offset in range(1, SHORT))
        lax.fori_loop(0, steps, featurize, held, unroll=8)


def queries(rows, last, products, conv, taps):
    steps, _, channels = conv.shape
    return pl.pallas_call(
        functools.partial(query_kernel, len(last)),
        out_shape=(pltpu.VMEM(conv.shape, jnp.float32),) * 2,
        in_specs=[VMEM] * (len(last) + 5),
        out_specs=(VMEM,) * 2,
        scratch_shapes=[segment_scratch(QUERY, steps * SEGMENTS, channels)],
        compiler_params=pltpu.CompilerParams(vmem_limit_bytes=8 * 1024 * 1024),
        name="queries",
    )(*in_vmem(rows, *last, *products, conv), taps)


def gate_kernel(
    where,
    query,
    gated,
    before,
    carried,
    decay,
    amplitude,
    power,
    keep,
    send,
    whole,
):
    core = where[2]
    steps, _, channels = query.shape
    length = keep.shape[0]
    modes = decay.shape[0]
    for low in range(0, channels, LANES):
        lanes = pl.ds(low, LANES)

        def spread(ref, *index):
            return jnp.broadcast_to(ref[(*index, lanes)].reshape(1, LANES), (SEGMENTS, LANES))

        decays = [spread(decay, mode) for mode in range(modes)]
        states = tuple(
            spread(amplitude, mode)
            * decays[mode]
            * (before[mode, :, lanes] + power[mode, :, lanes] * spread(carried, mode))
            for mode in range(modes)
        )

        def add(step, states):
            terms = list(states)
            while len(terms) > 1:
                terms = [terms[at] + terms[at + 1] for at in range(0, len(terms), 2)]
            whole[0, low // LANES, pl.ds(step, SEGMENTS, stride=steps + BEFORE), :] = (
                gated[step, :, lanes] + query[step, :, lanes] * terms[0]
            )
            return tuple(decays[mode] * states[mode] for mode in range(modes))

        lax.fori_loop(0, steps, add, states, unroll=8)
    for group in range(channels // LANES):
        lanes = pl.ds(group * LANES, LANES)
        for out, block in ((keep, core), (send, 1 - core)):
            for segment in range(SEGMENTS // CORES):
                first = (block * (SEGMENTS // CORES) + segment) * (steps + BEFORE)
                first = pl.multiple_of(first, SEGMENTS)
                out[pl.ds(segment * steps, steps), lanes] = whole[
                    0, group, pl.ds(first, steps), :
                ].astype(jnp.bfloat16)


def carry_gated(where, query, gated, before, carried, decay, amplitude, power):
    steps, _, channels = query.shape
    length = steps * SEGMENTS // 2
    return pl.pallas_call(
        gate_kernel,
        out_shape=(jax.ShapeDtypeStruct((length, channels), jnp.bfloat16),) * 2,
        in_specs=[SMEM] + [VMEM] * 7,
        out_specs=(VMEM,) * 2,
        scratch_shapes=[segment_scratch(QUERY, 2 * length, channels)],
        compiler_params=pltpu.CompilerParams(vmem_limit_bytes=8 * 1024 * 1024),
        name="gated",
    )(where, *in_vmem(query, gated, before), carried, decay, amplitude, power)


def carry_factors(rate, x, z, span):
    x, z = x.astype(jnp.float32), z.astype(jnp.float32)

    def after(tokens):
        return jnp.exp(-rate * tokens)

    def if_before(position, steps):
        return jnp.where(position >= steps, 1.0, 0.0)

    line = [after(span * (Z - 1 - z))]
    for steps in range(1, Z):
        source = jnp.where(z >= steps, z - steps, z - steps + Z)
        line.append(after(span * (Z - 1 - source)))
    near = [if_before(z, steps) * after(float(span * (steps - 1))) for steps in range(1, Z)]
    far = [
        if_before(x, steps) * after(span * (Z * (steps - 1) + z)) for steps in range(1, X)
    ]
    return jnp.stack(line + near + far)


def carried_states(ends, factors):
    line, near, far = factors[:Z], factors[Z : 2 * Z - 1], factors[2 * Z - 1 :]
    others = [along_z(ends, steps) for steps in range(1, Z)]
    total, carry = line[0] * ends, 0.0
    for at, state in enumerate(others):
        total = total + line[at + 1] * state
        carry = carry + near[at] * state
    for at, state in enumerate([along_x(total, steps) for steps in range(1, X)]):
        carry = carry + far[at] * state
    return carry


def local(tokens, in_weight, short_filter, residues, rates, skip):
    index = lax.axis_index("seq")
    core = index % CORES
    z = index // CORES % Z
    x = index // (CORES * Z)
    where = jnp.stack([x, z, core]).astype(jnp.int32)
    length = tokens.shape[0]
    channels = skip.shape[0]
    half = channels // 2
    span = CORES * length
    first = core == 0

    def half_of(array, axis):
        return lax.dynamic_slice_in_dim(array, core * half, half, axis)

    low, high = in_weight[:, :, :half], in_weight[:, :, half:]
    own = jnp.where(first, low, high)
    received, later_tokens = together(swap_cores(jnp.where(first, high, low)), tokens)
    block = jnp.concatenate(
        [jnp.where(first, own, received), jnp.where(first, received, own)], axis=1
    )
    beside = across_z(block, 1)
    right, left = sides(block)
    other = swap_cores(later_tokens)
    held, tail = together(block, later_tokens[length - HALO :])
    held, other_tail = together(held, swap_cores(tail))
    over = across_z(held, 2)
    halo = next_chip(jnp.where(first, other_tail, tail))
    beside, right, left, other, *parameters = together(
        beside, right, left, other, rates, residues, short_filter, skip
    )
    rates, residues, short_filter, skip = parameters
    both = (tokens, other)

    rate = half_of(rates, 0).T
    residue = half_of(residues, 0).T
    decay = jnp.exp(-rate)
    amplitude = residue * jnp.sqrt(-jnp.expm1(-2.0 * rate))
    step = span // SEGMENTS
    power = jnp.stack([jnp.exp(-rate * (step * distance)) for distance in (1, 2, 4)])
    starts = jnp.arange(SEGMENTS, dtype=jnp.float32)[None, :, None] * step
    start_power = jnp.exp(-rate[:, None, :] * starts)
    factors = carry_factors(rate, x, z, span)
    taps = half_of(short_filter, 2)
    direct = half_of(skip, 0)[None, :]

    far = forwards(right, left)
    pieces = with_sides(0, block, right, left)
    products = partial_products(where, pieces, both, (halo,), (), "first")
    right, left = sides(beside)
    right, left, *far, over, products, halo_products = together(
        right, left, *far, over, *products
    )

    opposite = across_z(over, 1)
    far_beside = across_z(far[0], 1), across_z(far[1], 1)
    pieces = with_sides(1, beside, right, left) + with_far(0, *far)
    products = partial_products(
        where, pieces, both, (halo,), (products, halo_products), "second"
    )
    right, left = sides(over)
    right, left, products, halo_products = together(right, left, *products)

    far = forwards(right, left)
    pieces = with_sides(2, over, right, left)
    products = partial_products(where, pieces, both, (halo,), (products, halo_products), "third")
    far_right, far_left, opposite, *far_beside, products, halo_products = together(
        *far, opposite, *far_beside, *products
    )

    right, left = sides(opposite)
    far_opposite = across_z(far_right, 1), across_z(far_left, 1)
    pieces = with_sides(3, opposite) + with_far(1, *far_beside) + with_far(2, far_right, far_left)
    *products, rows = partial_products(
        where,
        pieces,
        both,
        (halo,),
        (products, halo_products),
        "fourth",
        ((1, 3), (3, 3), (2, 3)),
    )
    small = (power, start_power, factors, decay, amplitude, taps, direct)
    *last, products, halo_products, rows, power, start_power, factors, decay, amplitude, taps, direct = (
        together(right, left, *far_opposite, *products, rows, *small)
    )
    products = products, halo_products

    conv, before, ends = signals(
        rows, last, products, taps, decay, amplitude, power, direct
    )
    query, product = queries(rows, last, products, conv, taps)
    carried = carried_states(ends, factors)
    keep, send = carry_gated(
        where, query, product, before, carried, decay, amplitude, start_power
    )
    taken = swap_cores(send)
    return jnp.concatenate(
        [jnp.where(first, keep, taken), jnp.where(first, taken, keep)], axis=1
    )


def solution(mesh):
    placed = (
        P("seq", None),
        P(None, "seq", "mp"),
        P(None, None, "mp"),
        P("mp", None),
        P("mp", None),
        P("mp"),
    )
    return jax.shard_map(
        local, mesh=mesh, in_specs=placed, out_specs=P("seq", "mp"), check_vma=False
    )
```

```python
import functools
import math

import jax
import jax.numpy as jnp
from jax import lax
from jax.experimental import pallas as pl
from jax.experimental.pallas import tpu as pltpu
from jax.sharding import PartitionSpec as P

SHORT = 7
X, Z, CORES = 4, 4, 2
CHIPS = X * Z
HALO = 16
LANES = 128
SEGMENTS = 8
BEFORE = 8

QUERY = pl.ds(0, 1)
KEY_VALUE = pl.ds(1, 2)
ALL = pl.ds(0, 3)

ANY = pl.BlockSpec(memory_space=pl.ANY)
HBM = pl.BlockSpec(memory_space=pltpu.HBM)
VMEM = pl.BlockSpec(memory_space=pltpu.VMEM)
SMEM = pl.BlockSpec(memory_space=pltpu.SMEM)


def in_hbm(*arrays):
    return [pltpu.with_memory_space_constraint(array, pltpu.HBM) for array in arrays]


def in_vmem(*arrays):
    return [pltpu.with_memory_space_constraint(array, pltpu.VMEM) for array in arrays]


def place(x, z, core):
    return (x * Z + z) * CORES + core


def permute(value, target):
    pairs = []
    for x in range(X):
        for z in range(Z):
            for core in range(CORES):
                to = target(x, z, core)
                if to is not None:
                    pairs.append((place(x, z, core), place(*to)))
    return lax.ppermute(value, "seq", pairs)


def along_x(value, steps):
    return permute(value, lambda x, z, core: ((x + steps) % X, z, core))


def along_z(value, steps):
    return permute(value, lambda x, z, core: (x, (z + steps) % Z, core))


def across_z(value, mask):
    return permute(value, lambda x, z, core: (x, z ^ mask, core))


def swap_cores(value):
    return permute(value, lambda x, z, core: (x, z, 1 - core))


def next_chip(value):
    def target(x, z, core):
        chip = x * Z + z + 1
        return (chip // Z, chip % Z, core) if chip < CHIPS else None

    return permute(value, target)


def together(*values):
    return lax.optimization_barrier(values)


def halves_kernel(right, left, right_half, left_half, sems):
    half = right_half.shape[1]
    copies = [
        pltpu.make_async_copy(right.at[:, pl.ds(0, half), :], right_half, sems.at[0]),
        pltpu.make_async_copy(left.at[:, pl.ds(half, half), :], left_half, sems.at[1]),
    ]
    for copy in copies:
        copy.start()
    for copy in copies:
        copy.wait()


def forwards(right, left):
    streams, height, channels = right.shape
    half = pltpu.VMEM((streams, height // 2, channels), right.dtype)
    right, left = pl.pallas_call(
        halves_kernel,
        out_shape=(half, half),
        in_specs=[ANY] * 2,
        out_specs=(VMEM,) * 2,
        scratch_shapes=[pltpu.SemaphoreType.DMA((2,))],
        compiler_params=pltpu.CompilerParams(vmem_limit_bytes=2 * 1024 * 1024),
        name="halves",
    )(right, left)
    return along_x(right, 1), along_x(left, 3)


def sides(block):
    return along_x(block, 1), along_x(block, 3)


def with_sides(z_mask, block, *both_sides):
    height = block.shape[1]
    return [
        (x_steps, z_mask, 0, array, 0, height)
        for x_steps, array in zip((0, 1, 3), (block, *both_sides))
    ]


def with_far(z_mask, far_right, far_left):
    height = far_right.shape[1]
    return [(2, z_mask, 0, far_right, 0, height), (2, z_mask, height, far_left, 0, height)]


def rounded(value):
    return value.astype(jnp.bfloat16).astype(jnp.float32)


def start_copies(plan, streams, where, pieces, mine, other, halo, rows, weights, sems):
    x, z, core = where[0], where[1], where[2]
    parts = []
    if halo is not None:
        parts.append((1, halo, 0))
    if mine is not None:
        base = HALO if halo is not None else 0
        length = mine.shape[0]
        parts += [(2, mine, base + core * length), (3, other, base + (1 - core) * length)]
    depth = CHIPS * 2 * LANES
    copies = []
    offset = 0
    for at, (x_steps, z_mask, row, which, start, height) in enumerate(plan):
        chip = (x - x_steps + X) % X * Z + (z ^ z_mask)
        column = pl.multiple_of(chip * (depth // CHIPS) + row, LANES)
        copies.append(
            pltpu.make_async_copy(
                pieces[which].at[streams, pl.ds(start, height), :],
                weights.at[:, pl.ds(offset, height), :],
                sems.at[at, 0],
            )
        )
        for sem, array, first in parts:
            if array is not halo:
                first = pl.multiple_of(first, HALO)
            copies.append(
                pltpu.make_async_copy(
                    array.at[:, pl.ds(column, height)],
                    rows.at[pl.ds(first, array.shape[0]), pl.ds(offset, height)],
                    sems.at[at, sem],
                )
            )
        offset += height
    for copy in copies:
        copy.start()
    return copies


def columns_to(rows, where, chips, mine, other, halo, sems):
    x, z, core = where[0], where[1], where[2]
    length, width = mine.shape[0], 2 * LANES
    copies = []
    for at, (x_steps, z_mask) in enumerate(chips):
        chip = (x - x_steps + X) % X * Z + (z ^ z_mask)
        span = pl.ds(pl.multiple_of(chip * width, LANES), width)
        into = pl.ds(at * width, width)
        for sem, array, first in (
            (0, halo, 0),
            (1, mine, HALO + core * length),
            (2, other, HALO + (1 - core) * length),
        ):
            first = first if sem == 0 else pl.multiple_of(first, HALO)
            copies.append(
                pltpu.make_async_copy(
                    array.at[:, span],
                    rows.at[pl.ds(first, array.shape[0]), into],
                    sems.at[at, sem],
                )
            )
    for copy in copies:
        copy.start()
    return copies


def multiply(rows, weights, finish):
    for stream, weight in enumerate(weights):
        channels = weight.shape[1]
        product = jnp.dot(rows[...], weight, preferred_element_type=jnp.float32)
        for group in range(channels // LANES):
            finish(stream, group, product[:, group * LANES : (group + 1) * LANES])


def segmented(ref, before, halo_before, first_stream):
    stride = ref.shape[2] // SEGMENTS
    steps = stride - BEFORE

    def finish(stream, group, share):
        main = rounded(before[first_stream + stream, group] + share[HALO:])
        head = rounded(halo_before[first_stream + stream, group] + share[:HALO])
        ref[stream, group, 0:BEFORE, :] = head[HALO - BEFORE :]
        ref[stream, group, BEFORE:stride, :] = main[:steps]
        for segment in range(1, SEGMENTS):
            first = segment * steps - BEFORE
            ref[stream, group, segment * stride : (segment + 1) * stride, :] = main[
                first : first + stride
            ]

    def load(stream, group, step):
        return ref[stream, group, pl.ds(BEFORE + step, SEGMENTS, stride=stride), :]

    return finish, load


def segment_scratch(streams, rows, channels):
    return pltpu.VMEM((streams.size, channels // LANES, rows + SEGMENTS * BEFORE, LANES), jnp.float32)


def arrays_in(plan):
    return 1 + max(step[3] for step in plan)


def partial_kernel(plan, has_main, has_halo, has_before, kept_from, where, *refs):
    count = arrays_in(plan)
    pieces, refs = refs[:count], list(refs[count:])
    mine, other = (refs.pop(0), refs.pop(0)) if has_main else (None, None)
    halo = refs.pop(0) if has_halo else None
    before = refs.pop(0) if has_main and has_before else None
    halo_before = refs.pop(0) if has_halo and has_before else None
    totals = refs.pop(0) if has_main else None
    halo_totals = refs.pop(0) if has_halo else None
    kept = refs.pop(0) if kept_from else None
    rows, weights, sems, kept_sems = refs
    copies = start_copies(plan, ALL, where, pieces, mine, other, halo, rows, weights, sems)
    kept_copies = (
        columns_to(kept, where, kept_from, mine, other, halo, kept_sems) if kept_from else []
    )

    def finish(stream, group, share):
        if has_halo:
            head = share[:HALO]
            halo_totals[stream, group] = (
                head if halo_before is None else halo_before[stream, group] + head
            )
            share = share[HALO:]
        if has_main:
            totals[stream, group] = share if before is None else before[stream, group] + share

    for copy in copies:
        copy.wait()
    multiply(rows, [weights[stream] for stream in range(ALL.size)], finish)
    for copy in kept_copies:
        copy.wait()


def plan_of(pieces):
    arrays = []
    plan = []
    for x_steps, z_mask, row, array, start, height in pieces:
        which = next((at for at, seen in enumerate(arrays) if seen is array), len(arrays))
        if which == len(arrays):
            arrays.append(array)
        plan.append((x_steps, z_mask, row, which, start, height))
    return tuple(plan), arrays, sum(step[-1] for step in plan)


def copy_scratch(pieces, streams, rows):
    plan, arrays, depth = plan_of(pieces)
    channels = arrays[0].shape[2]
    return [
        pltpu.VMEM((rows, depth), jnp.bfloat16),
        pltpu.VMEM((streams.size, depth, channels), jnp.bfloat16),
        pltpu.SemaphoreType.DMA((len(plan), 4)),
        pltpu.SemaphoreType.DMA((4, 3)),
    ]


def partial_products(where, pieces, tokens, halo, before, name, kept_from=None):
    plan, arrays, _ = plan_of(pieces)
    channels = arrays[0].shape[2]
    heights = [sum(array.shape[0] for array in tokens)] if tokens else []
    heights += [HALO] if halo else []
    shapes = [
        pltpu.VMEM((ALL.size, channels // LANES, height, LANES), jnp.float32) for height in heights
    ]
    if kept_from:
        shapes.append(pltpu.VMEM((sum(heights), len(kept_from) * 2 * LANES), jnp.bfloat16))
    inputs = [*arrays, *tokens, *halo]
    return pl.pallas_call(
        functools.partial(
            partial_kernel, plan, bool(tokens), bool(halo), bool(before), kept_from
        ),
        out_shape=shapes,
        in_specs=[SMEM] + [HBM] * len(inputs) + [VMEM] * len(before),
        out_specs=[VMEM] * len(shapes),
        scratch_shapes=copy_scratch(pieces, ALL, sum(heights)),
        compiler_params=pltpu.CompilerParams(vmem_limit_bytes=12 * 1024 * 1024),
        name=name,
    )(where, *in_hbm(*inputs), *in_vmem(*before))


def last_weights(last, streams):
    return [
        jnp.concatenate([array[stream] for array in last], axis=0)
        for stream in range(streams.start, streams.start + streams.size)
    ]


def signal_kernel(count, rows, *refs):
    last, refs = refs[:count], refs[count:]
    products, halo_products, taps, decay, amplitude, power, skip = refs[:7]
    signal, before, ends, projected = refs[7:]
    channels = last[0].shape[2]
    steps = signal.shape[0]
    finish, load = segmented(projected, products, halo_products, KEY_VALUE.start)
    multiply(rows, last_weights(last, KEY_VALUE), finish)
    for low in range(0, channels, LANES):
        lanes = pl.ds(low, LANES)
        group = low // LANES

        def spread(ref, *index):
            return jnp.broadcast_to(ref[(*index, lanes)].reshape(1, LANES), (SEGMENTS, LANES))

        key_taps = [spread(taps, 1, offset) for offset in range(SHORT)]
        value_taps = [spread(taps, 2, offset) for offset in range(SHORT)]

        def featurize(step, carry):
            keys, values = carry
            keys = (load(0, group, step),) + keys
            values = (load(1, group, step),) + values
            total_key = key_taps[0] * keys[0]
            total_value = value_taps[0] * values[0]
            for offset in range(1, SHORT):
                total_key += key_taps[offset] * keys[offset]
                total_value += value_taps[offset] * values[offset]
            signal[step, :, lanes] = total_key * total_value
            return keys[:-1], values[:-1]

        lax.fori_loop(
            0,
            steps,
            featurize,
            (
                tuple(load(0, group, -offset) for offset in range(1, SHORT)),
                tuple(load(1, group, -offset) for offset in range(1, SHORT)),
            ),
            unroll=8,
        )
        modes = decay.shape[0]
        decays = [spread(decay, mode) for mode in range(modes)]
        amplitudes = [spread(amplitude, mode) for mode in range(modes)]
        direct = spread(skip, 0)

        def scan(step, states):
            here = signal[step, :, lanes]
            states = tuple(decays[mode] * states[mode] + here for mode in range(modes))
            terms = [amplitudes[mode] * states[mode] for mode in range(modes)]
            while len(terms) > 1:
                terms = [terms[at] + terms[at + 1] for at in range(0, len(terms), 2)]
            signal[step, :, lanes] = terms[0] + direct * here
            return states

        empty = jnp.zeros((SEGMENTS, LANES), jnp.float32)
        states = lax.fori_loop(0, steps, scan, (empty,) * modes, unroll=8)
        segment = lax.broadcasted_iota(jnp.int32, (SEGMENTS, LANES), 0)
        for mode in range(modes):
            state = states[mode]
            for level, distance in enumerate((1, 2, 4)):
                moved = pltpu.roll(state, distance, 0)
                state = state + jnp.where(
                    segment >= distance, spread(power, level, mode) * moved, 0.0
                )
            before[mode, :, lanes] = jnp.where(segment >= 1, pltpu.roll(state, 1, 0), 0.0)
            ends[pl.ds(mode, 1), lanes] = state[SEGMENTS - 1 :, :]


def signals(rows, last, products, taps, decay, amplitude, power, skip):
    modes, channels = decay.shape
    length = rows.shape[0] - HALO
    return pl.pallas_call(
        functools.partial(signal_kernel, len(last)),
        out_shape=(
            pltpu.VMEM((length // SEGMENTS, SEGMENTS, channels), jnp.float32),
            pltpu.VMEM((modes, SEGMENTS, channels), jnp.float32),
            jax.ShapeDtypeStruct((modes, channels), jnp.float32),
        ),
        in_specs=[VMEM] * (len(last) + 8),
        out_specs=(VMEM,) * 3,
        scratch_shapes=[segment_scratch(KEY_VALUE, length, channels)],
        compiler_params=pltpu.CompilerParams(vmem_limit_bytes=8 * 1024 * 1024),
        name="signals",
    )(*in_vmem(rows, *last, *products), taps, decay, amplitude, power, skip)


def query_kernel(count, rows, *refs):
    last, refs = refs[:count], refs[count:]
    products, halo_products, conv, taps, query, gated, projected = refs
    channels = last[0].shape[2]
    steps = conv.shape[0]
    finish, load = segmented(projected, products, halo_products, QUERY.start)
    multiply(rows, last_weights(last, QUERY), finish)
    for group in range(channels // LANES):
        lanes = pl.ds(group * LANES, LANES)
        spread = [
            jnp.broadcast_to(taps[0, offset, lanes].reshape(1, LANES), (SEGMENTS, LANES))
            for offset in range(SHORT)
        ]

        def featurize(step, held):
            held = (load(0, group, step),) + held
            total = spread[0] * held[0]
            for offset in range(1, SHORT):
                total += spread[offset] * held[offset]
            query[step, :, lanes] = total
            gated[step, :, lanes] = total * conv[step, :, lanes]
            return held[:-1]

        held = tuple(load(0, group, -offset) for offset in range(1, SHORT))
        lax.fori_loop(0, steps, featurize, held, unroll=8)


def queries(rows, last, products, conv, taps):
    steps, _, channels = conv.shape
    return pl.pallas_call(
        functools.partial(query_kernel, len(last)),
        out_shape=(pltpu.VMEM(conv.shape, jnp.float32),) * 2,
        in_specs=[VMEM] * (len(last) + 5),
        out_specs=(VMEM,) * 2,
        scratch_shapes=[segment_scratch(QUERY, steps * SEGMENTS, channels)],
        compiler_params=pltpu.CompilerParams(vmem_limit_bytes=8 * 1024 * 1024),
        name="queries",
    )(*in_vmem(rows, *last, *products, conv), taps)


def gate_kernel(
    where,
    query,
    gated,
    before,
    carried,
    decay,
    amplitude,
    power,
    keep,
    send,
    whole,
):
    core = where[2]
    steps, _, channels = query.shape
    length = keep.shape[0]
    modes = decay.shape[0]
    for low in range(0, channels, LANES):
        lanes = pl.ds(low, LANES)

        def spread(ref, *index):
            return jnp.broadcast_to(ref[(*index, lanes)].reshape(1, LANES), (SEGMENTS, LANES))

        decays = [spread(decay, mode) for mode in range(modes)]
        states = tuple(
            spread(amplitude, mode)
            * decays[mode]
            * (before[mode, :, lanes] + power[mode, :, lanes] * spread(carried, mode))
            for mode in range(modes)
        )

        def add(step, states):
            terms = list(states)
            while len(terms) > 1:
                terms = [terms[at] + terms[at + 1] for at in range(0, len(terms), 2)]
            whole[0, low // LANES, pl.ds(step, SEGMENTS, stride=steps + BEFORE), :] = (
                gated[step, :, lanes] + query[step, :, lanes] * terms[0]
            )
            return tuple(decays[mode] * states[mode] for mode in range(modes))

        lax.fori_loop(0, steps, add, states, unroll=8)
    for group in range(channels // LANES):
        lanes = pl.ds(group * LANES, LANES)
        for out, block in ((keep, core), (send, 1 - core)):
            for segment in range(SEGMENTS // CORES):
                first = (block * (SEGMENTS // CORES) + segment) * (steps + BEFORE)
                first = pl.multiple_of(first, SEGMENTS)
                out[pl.ds(segment * steps, steps), lanes] = whole[
                    0, group, pl.ds(first, steps), :
                ].astype(jnp.bfloat16)


def carry_gated(where, query, gated, before, carried, decay, amplitude, power):
    steps, _, channels = query.shape
    length = steps * SEGMENTS // 2
    return pl.pallas_call(
        gate_kernel,
        out_shape=(jax.ShapeDtypeStruct((length, channels), jnp.bfloat16),) * 2,
        in_specs=[SMEM] + [VMEM] * 7,
        out_specs=(VMEM,) * 2,
        scratch_shapes=[segment_scratch(QUERY, 2 * length, channels)],
        compiler_params=pltpu.CompilerParams(vmem_limit_bytes=8 * 1024 * 1024),
        name="gated",
    )(where, *in_vmem(query, gated, before), carried, decay, amplitude, power)


def carry_factors(rate, x, z, span):
    x, z = x.astype(jnp.float32), z.astype(jnp.float32)

    def after(tokens):
        return jnp.exp(-rate * tokens)

    def if_before(position, steps):
        return jnp.where(position >= steps, 1.0, 0.0)

    line = [after(span * (Z - 1 - z))]
    for steps in range(1, Z):
        source = jnp.where(z >= steps, z - steps, z - steps + Z)
        line.append(after(span * (Z - 1 - source)))
    near = [if_before(z, steps) * after(float(span * (steps - 1))) for steps in range(1, Z)]
    far = [
        if_before(x, steps) * after(span * (Z * (steps - 1) + z)) for steps in range(1, X)
    ]
    return jnp.stack(line + near + far)


def carried_states(ends, factors):
    line, near, far = factors[:Z], factors[Z : 2 * Z - 1], factors[2 * Z - 1 :]
    others = [along_z(ends, steps) for steps in range(1, Z)]
    total, carry = line[0] * ends, 0.0
    for at, state in enumerate(others):
        total = total + line[at + 1] * state
        carry = carry + near[at] * state
    for at, state in enumerate([along_x(total, steps) for steps in range(1, X)]):
        carry = carry + far[at] * state
    return carry


def local(tokens, in_weight, short_filter, residues, rates, skip):
    index = lax.axis_index("seq")
    core = index % CORES
    z = index // CORES % Z
    x = index // (CORES * Z)
    where = jnp.stack([x, z, core]).astype(jnp.int32)
    length = tokens.shape[0]
    channels = skip.shape[0]
    half = channels // 2
    span = CORES * length
    first = core == 0

    def half_of(array, axis):
        return lax.dynamic_slice_in_dim(array, core * half, half, axis)

    low, high = in_weight[:, :, :half], in_weight[:, :, half:]
    received, later_tokens = together(swap_cores(jnp.where(first, high, low)), tokens)
    block = jnp.concatenate(
        [jnp.where(first, low, received), jnp.where(first, received, high)], axis=1
    )

    beside = across_z(block, 1)
    right, left = sides(block)
    other = swap_cores(later_tokens)
    held, late_tokens = together(block, later_tokens)
    tail = late_tokens[length - HALO :]
    held, other_tail = together(held, swap_cores(tail))
    over = across_z(held, 2)
    halo = next_chip(jnp.where(first, other_tail, tail))
    beside, right, left, other, *parameters = together(
        beside, right, left, other, rates, residues, short_filter, skip
    )
    rates, residues, short_filter, skip = parameters
    both = (tokens, other)

    rate = half_of(rates, 0).T
    residue = half_of(residues, 0).T
    decay = jnp.exp(-rate)
    amplitude = residue * jnp.sqrt(-jnp.expm1(-2.0 * rate))
    step = span // SEGMENTS
    power = jnp.stack([jnp.exp(-rate * (step * distance)) for distance in (1, 2, 4)])
    starts = jnp.arange(SEGMENTS, dtype=jnp.float32)[None, :, None] * step
    start_power = jnp.exp(-rate[:, None, :] * starts)
    factors = carry_factors(rate, x, z, span)
    taps = half_of(short_filter, 2)
    direct = half_of(skip, 0)[None, :]

    far = forwards(right, left)
    pieces = with_sides(0, block, right, left)
    products = partial_products(where, pieces, both, (halo,), (), "first")
    right, left = sides(beside)
    right, left, *far, over, products, halo_products = together(
        right, left, *far, over, *products
    )

    opposite = across_z(over, 1)
    far_beside = across_z(far[0], 1), across_z(far[1], 1)
    pieces = with_sides(1, beside, right, left) + with_far(0, *far)
    products = partial_products(
        where, pieces, both, (halo,), (products, halo_products), "second"
    )
    right, left = sides(over)
    right, left, products, halo_products = together(right, left, *products)

    pieces = with_sides(2, over, right, left)
    far = forwards(right, left)
    right, left = sides(opposite)
    far_opposite = across_z(far[0], 1), across_z(far[1], 1)
    pieces += with_sides(3, opposite) + with_far(2, *far)
    *products, rows = partial_products(
        where,
        pieces,
        both,
        (halo,),
        (products, halo_products),
        "third",
        ((1, 3), (3, 3), (2, 3), (2, 1)),
    )
    small = (power, start_power, factors, decay, amplitude, taps, direct)
    *last, products, halo_products, rows, power, start_power, factors, decay, amplitude, taps, direct = (
        together(right, left, *far_opposite, *far_beside, *products, rows, *small)
    )
    products = products, halo_products

    conv, before, ends = signals(
        rows, last, products, taps, decay, amplitude, power, direct
    )
    query, product = queries(rows, last, products, conv, taps)
    carried = carried_states(ends, factors)
    keep, send = carry_gated(
        where, query, product, before, carried, decay, amplitude, start_power
    )
    taken = swap_cores(send)
    return jnp.concatenate(
        [jnp.where(first, keep, taken), jnp.where(first, taken, keep)], axis=1
    )


def solution(mesh):
    placed = (
        P("seq", None),
        P(None, "seq", "mp"),
        P(None, None, "mp"),
        P("mp", None),
        P("mp", None),
        P("mp"),
    )
    return jax.shard_map(
        local, mesh=mesh, in_specs=placed, out_specs=P("seq", "mp"), check_vma=False
    )
```

```python
import functools
import math

import jax
import jax.numpy as jnp
from jax import lax
from jax.experimental import pallas as pl
from jax.experimental.pallas import tpu as pltpu
from jax.sharding import PartitionSpec as P

SHORT = 7
X, Z, CORES = 4, 4, 2
CHIPS = X * Z
HALO = 16
LANES = 128
SEGMENTS = 8
BEFORE = 8

QUERY = pl.ds(0, 1)
KEY_VALUE = pl.ds(1, 2)
ALL = pl.ds(0, 3)

ANY = pl.BlockSpec(memory_space=pl.ANY)
HBM = pl.BlockSpec(memory_space=pltpu.HBM)
VMEM = pl.BlockSpec(memory_space=pltpu.VMEM)
SMEM = pl.BlockSpec(memory_space=pltpu.SMEM)


def in_hbm(*arrays):
    return [pltpu.with_memory_space_constraint(array, pltpu.HBM) for array in arrays]


def in_vmem(*arrays):
    return [pltpu.with_memory_space_constraint(array, pltpu.VMEM) for array in arrays]


def place(x, z, core):
    return (x * Z + z) * CORES + core


def permute(value, target):
    pairs = []
    for x in range(X):
        for z in range(Z):
            for core in range(CORES):
                to = target(x, z, core)
                if to is not None:
                    pairs.append((place(x, z, core), place(*to)))
    return lax.ppermute(value, "seq", pairs)


def along_x(value, steps):
    return permute(value, lambda x, z, core: ((x + steps) % X, z, core))


def along_z(value, steps):
    return permute(value, lambda x, z, core: (x, (z + steps) % Z, core))


def across_z(value, mask):
    return permute(value, lambda x, z, core: (x, z ^ mask, core))


def swap_cores(value):
    return permute(value, lambda x, z, core: (x, z, 1 - core))


def next_chip(value):
    def target(x, z, core):
        chip = x * Z + z + 1
        return (chip // Z, chip % Z, core) if chip < CHIPS else None

    return permute(value, target)


def together(*values):
    return lax.optimization_barrier(values)


def halves_kernel(right, left, right_half, left_half, sems):
    half = right_half.shape[1]
    copies = [
        pltpu.make_async_copy(right.at[:, pl.ds(0, half), :], right_half, sems.at[0]),
        pltpu.make_async_copy(left.at[:, pl.ds(half, half), :], left_half, sems.at[1]),
    ]
    for copy in copies:
        copy.start()
    for copy in copies:
        copy.wait()


def forwards(right, left):
    streams, height, channels = right.shape
    half = pltpu.VMEM((streams, height // 2, channels), right.dtype)
    right, left = pl.pallas_call(
        halves_kernel,
        out_shape=(half, half),
        in_specs=[ANY] * 2,
        out_specs=(VMEM,) * 2,
        scratch_shapes=[pltpu.SemaphoreType.DMA((2,))],
        compiler_params=pltpu.CompilerParams(vmem_limit_bytes=2 * 1024 * 1024),
        name="halves",
    )(right, left)
    return along_x(right, 1), along_x(left, 3)


def sides(block):
    return along_x(block, 1), along_x(block, 3)


def with_sides(z_mask, block, *both_sides):
    height = block.shape[1]
    return [
        (x_steps, z_mask, 0, array, 0, height)
        for x_steps, array in zip((0, 1, 3), (block, *both_sides))
    ]


def with_far(z_mask, far_right, far_left):
    height = far_right.shape[1]
    return [(2, z_mask, 0, far_right, 0, height), (2, z_mask, height, far_left, 0, height)]


def rounded(value):
    return value.astype(jnp.bfloat16).astype(jnp.float32)


def start_copies(plan, streams, where, pieces, mine, other, halo, rows, weights, sems):
    x, z, core = where[0], where[1], where[2]
    parts = []
    if halo is not None:
        parts.append((1, halo, 0))
    if mine is not None:
        base = HALO if halo is not None else 0
        length = mine.shape[0]
        parts += [(2, mine, base + core * length), (3, other, base + (1 - core) * length)]
    depth = CHIPS * 2 * LANES
    copies = []
    offset = 0
    for at, (x_steps, z_mask, row, which, start, height) in enumerate(plan):
        chip = (x - x_steps + X) % X * Z + (z ^ z_mask)
        column = pl.multiple_of(chip * (depth // CHIPS) + row, LANES)
        copies.append(
            pltpu.make_async_copy(
                pieces[which].at[streams, pl.ds(start, height), :],
                weights.at[:, pl.ds(offset, height), :],
                sems.at[at, 0],
            )
        )
        for sem, array, first in parts:
            if array is not halo:
                first = pl.multiple_of(first, HALO)
            copies.append(
                pltpu.make_async_copy(
                    array.at[:, pl.ds(column, height)],
                    rows.at[pl.ds(first, array.shape[0]), pl.ds(offset, height)],
                    sems.at[at, sem],
                )
            )
        offset += height
    for copy in copies:
        copy.start()
    return copies


def columns_to(rows, where, chips, mine, other, halo, sems):
    x, z, core = where[0], where[1], where[2]
    length, width = mine.shape[0], 2 * LANES
    copies = []
    for at, (x_steps, z_mask) in enumerate(chips):
        chip = (x - x_steps + X) % X * Z + (z ^ z_mask)
        span = pl.ds(pl.multiple_of(chip * width, LANES), width)
        into = pl.ds(at * width, width)
        for sem, array, first in (
            (0, halo, 0),
            (1, mine, HALO + core * length),
            (2, other, HALO + (1 - core) * length),
        ):
            first = first if sem == 0 else pl.multiple_of(first, HALO)
            copies.append(
                pltpu.make_async_copy(
                    array.at[:, span],
                    rows.at[pl.ds(first, array.shape[0]), into],
                    sems.at[at, sem],
                )
            )
    for copy in copies:
        copy.start()
    return copies


def multiply(rows, weights, finish):
    for stream, weight in enumerate(weights):
        channels = weight.shape[1]
        product = jnp.dot(rows[...], weight, preferred_element_type=jnp.float32)
        for group in range(channels // LANES):
            finish(stream, group, product[:, group * LANES : (group + 1) * LANES])


def segmented(ref, before, halo_before, first_stream):
    stride = ref.shape[2] // SEGMENTS
    steps = stride - BEFORE

    def finish(stream, group, share):
        main = rounded(before[first_stream + stream, group] + share[HALO:])
        head = rounded(halo_before[first_stream + stream, group] + share[:HALO])
        ref[stream, group, 0:BEFORE, :] = head[HALO - BEFORE :]
        ref[stream, group, BEFORE:stride, :] = main[:steps]
        for segment in range(1, SEGMENTS):
            first = segment * steps - BEFORE
            ref[stream, group, segment * stride : (segment + 1) * stride, :] = main[
                first : first + stride
            ]

    def load(stream, group, step):
        return ref[stream, group, pl.ds(BEFORE + step, SEGMENTS, stride=stride), :]

    return finish, load


def segment_scratch(streams, rows, channels):
    return pltpu.VMEM((streams.size, channels // LANES, rows + SEGMENTS * BEFORE, LANES), jnp.float32)


def arrays_in(plan):
    return 1 + max(step[3] for step in plan)


def partial_kernel(plan, has_main, has_halo, has_before, kept_from, where, *refs):
    count = arrays_in(plan)
    pieces, refs = refs[:count], list(refs[count:])
    mine, other = (refs.pop(0), refs.pop(0)) if has_main else (None, None)
    halo = refs.pop(0) if has_halo else None
    before = refs.pop(0) if has_main and has_before else None
    halo_before = refs.pop(0) if has_halo and has_before else None
    totals = refs.pop(0) if has_main else None
    halo_totals = refs.pop(0) if has_halo else None
    kept = refs.pop(0) if kept_from else None
    rows, weights, sems, kept_sems = refs
    copies = start_copies(plan, ALL, where, pieces, mine, other, halo, rows, weights, sems)
    kept_copies = (
        columns_to(kept, where, kept_from, mine, other, halo, kept_sems) if kept_from else []
    )

    def finish(stream, group, share):
        if has_halo:
            head = share[:HALO]
            halo_totals[stream, group] = (
                head if halo_before is None else halo_before[stream, group] + head
            )
            share = share[HALO:]
        if has_main:
            totals[stream, group] = share if before is None else before[stream, group] + share

    for copy in copies:
        copy.wait()
    multiply(rows, [weights[stream] for stream in range(ALL.size)], finish)
    for copy in kept_copies:
        copy.wait()


def plan_of(pieces):
    arrays = []
    plan = []
    for x_steps, z_mask, row, array, start, height in pieces:
        which = next((at for at, seen in enumerate(arrays) if seen is array), len(arrays))
        if which == len(arrays):
            arrays.append(array)
        plan.append((x_steps, z_mask, row, which, start, height))
    return tuple(plan), arrays, sum(step[-1] for step in plan)


def copy_scratch(pieces, streams, rows):
    plan, arrays, depth = plan_of(pieces)
    channels = arrays[0].shape[2]
    return [
        pltpu.VMEM((rows, depth), jnp.bfloat16),
        pltpu.VMEM((streams.size, depth, channels), jnp.bfloat16),
        pltpu.SemaphoreType.DMA((len(plan), 4)),
        pltpu.SemaphoreType.DMA((4, 3)),
    ]


def partial_products(where, pieces, tokens, halo, before, name, kept_from=None):
    plan, arrays, _ = plan_of(pieces)
    channels = arrays[0].shape[2]
    heights = [sum(array.shape[0] for array in tokens)] if tokens else []
    heights += [HALO] if halo else []
    shapes = [
        pltpu.VMEM((ALL.size, channels // LANES, height, LANES), jnp.float32) for height in heights
    ]
    if kept_from:
        shapes.append(pltpu.VMEM((sum(heights), len(kept_from) * 2 * LANES), jnp.bfloat16))
    inputs = [*arrays, *tokens, *halo]
    return pl.pallas_call(
        functools.partial(
            partial_kernel, plan, bool(tokens), bool(halo), bool(before), kept_from
        ),
        out_shape=shapes,
        in_specs=[SMEM] + [HBM] * len(inputs) + [VMEM] * len(before),
        out_specs=[VMEM] * len(shapes),
        scratch_shapes=copy_scratch(pieces, ALL, sum(heights)),
        compiler_params=pltpu.CompilerParams(vmem_limit_bytes=12 * 1024 * 1024),
        name=name,
    )(where, *in_hbm(*inputs), *in_vmem(*before))


def last_weights(last, streams):
    return [
        jnp.concatenate([array[stream] for array in last], axis=0)
        for stream in range(streams.start, streams.start + streams.size)
    ]


def signal_kernel(count, rows, *refs):
    last, refs = refs[:count], refs[count:]
    products, halo_products, taps, decay, amplitude, power, skip = refs[:7]
    signal, before, ends, projected = refs[7:]
    channels = last[0].shape[2]
    steps = signal.shape[0]
    finish, load = segmented(projected, products, halo_products, KEY_VALUE.start)
    multiply(rows, last_weights(last, KEY_VALUE), finish)
    for low in range(0, channels, LANES):
        lanes = pl.ds(low, LANES)
        group = low // LANES

        def spread(ref, *index):
            return jnp.broadcast_to(ref[(*index, lanes)].reshape(1, LANES), (SEGMENTS, LANES))

        key_taps = [spread(taps, 1, offset) for offset in range(SHORT)]
        value_taps = [spread(taps, 2, offset) for offset in range(SHORT)]

        def featurize(step, carry):
            keys, values = carry
            keys = (load(0, group, step),) + keys
            values = (load(1, group, step),) + values
            total_key = key_taps[0] * keys[0]
            total_value = value_taps[0] * values[0]
            for offset in range(1, SHORT):
                total_key += key_taps[offset] * keys[offset]
                total_value += value_taps[offset] * values[offset]
            signal[step, :, lanes] = total_key * total_value
            return keys[:-1], values[:-1]

        lax.fori_loop(
            0,
            steps,
            featurize,
            (
                tuple(load(0, group, -offset) for offset in range(1, SHORT)),
                tuple(load(1, group, -offset) for offset in range(1, SHORT)),
            ),
            unroll=8,
        )
        modes = decay.shape[0]
        decays = [spread(decay, mode) for mode in range(modes)]
        amplitudes = [spread(amplitude, mode) for mode in range(modes)]
        direct = spread(skip, 0)

        def scan(step, states):
            here = signal[step, :, lanes]
            states = tuple(decays[mode] * states[mode] + here for mode in range(modes))
            terms = [amplitudes[mode] * states[mode] for mode in range(modes)]
            while len(terms) > 1:
                terms = [terms[at] + terms[at + 1] for at in range(0, len(terms), 2)]
            signal[step, :, lanes] = terms[0] + direct * here
            return states

        empty = jnp.zeros((SEGMENTS, LANES), jnp.float32)
        states = lax.fori_loop(0, steps, scan, (empty,) * modes, unroll=8)
        segment = lax.broadcasted_iota(jnp.int32, (SEGMENTS, LANES), 0)
        for mode in range(modes):
            state = states[mode]
            for level, distance in enumerate((1, 2, 4)):
                moved = pltpu.roll(state, distance, 0)
                state = state + jnp.where(
                    segment >= distance, spread(power, level, mode) * moved, 0.0
                )
            before[mode, :, lanes] = jnp.where(segment >= 1, pltpu.roll(state, 1, 0), 0.0)
            ends[pl.ds(mode, 1), lanes] = state[SEGMENTS - 1 :, :]


def signals(rows, last, products, taps, decay, amplitude, power, skip):
    modes, channels = decay.shape
    length = rows.shape[0] - HALO
    return pl.pallas_call(
        functools.partial(signal_kernel, len(last)),
        out_shape=(
            pltpu.VMEM((length // SEGMENTS, SEGMENTS, channels), jnp.float32),
            pltpu.VMEM((modes, SEGMENTS, channels), jnp.float32),
            jax.ShapeDtypeStruct((modes, channels), jnp.float32),
        ),
        in_specs=[VMEM] * (len(last) + 8),
        out_specs=(VMEM,) * 3,
        scratch_shapes=[segment_scratch(KEY_VALUE, length, channels)],
        compiler_params=pltpu.CompilerParams(vmem_limit_bytes=8 * 1024 * 1024),
        name="signals",
    )(*in_vmem(rows, *last, *products), taps, decay, amplitude, power, skip)


def query_kernel(count, rows, *refs):
    last, refs = refs[:count], refs[count:]
    products, halo_products, conv, taps, query, gated, projected = refs
    channels = last[0].shape[2]
    steps = conv.shape[0]
    finish, load = segmented(projected, products, halo_products, QUERY.start)
    multiply(rows, last_weights(last, QUERY), finish)
    for group in range(channels // LANES):
        lanes = pl.ds(group * LANES, LANES)
        spread = [
            jnp.broadcast_to(taps[0, offset, lanes].reshape(1, LANES), (SEGMENTS, LANES))
            for offset in range(SHORT)
        ]

        def featurize(step, held):
            held = (load(0, group, step),) + held
            total = spread[0] * held[0]
            for offset in range(1, SHORT):
                total += spread[offset] * held[offset]
            query[step, :, lanes] = total
            gated[step, :, lanes] = total * conv[step, :, lanes]
            return held[:-1]

        held = tuple(load(0, group, -offset) for offset in range(1, SHORT))
        lax.fori_loop(0, steps, featurize, held, unroll=8)


def queries(rows, last, products, conv, taps):
    steps, _, channels = conv.shape
    return pl.pallas_call(
        functools.partial(query_kernel, len(last)),
        out_shape=(pltpu.VMEM(conv.shape, jnp.float32),) * 2,
        in_specs=[VMEM] * (len(last) + 5),
        out_specs=(VMEM,) * 2,
        scratch_shapes=[segment_scratch(QUERY, steps * SEGMENTS, channels)],
        compiler_params=pltpu.CompilerParams(vmem_limit_bytes=8 * 1024 * 1024),
        name="queries",
    )(*in_vmem(rows, *last, *products, conv), taps)


def gate_kernel(
    where,
    query,
    gated,
    before,
    carried,
    decay,
    amplitude,
    power,
    keep,
    send,
    whole,
):
    core = where[2]
    steps, _, channels = query.shape
    length = keep.shape[0]
    modes = decay.shape[0]
    for low in range(0, channels, LANES):
        lanes = pl.ds(low, LANES)

        def spread(ref, *index):
            return jnp.broadcast_to(ref[(*index, lanes)].reshape(1, LANES), (SEGMENTS, LANES))

        decays = [spread(decay, mode) for mode in range(modes)]
        states = tuple(
            spread(amplitude, mode)
            * decays[mode]
            * (before[mode, :, lanes] + power[mode, :, lanes] * spread(carried, mode))
            for mode in range(modes)
        )

        def add(step, states):
            terms = list(states)
            while len(terms) > 1:
                terms = [terms[at] + terms[at + 1] for at in range(0, len(terms), 2)]
            whole[0, low // LANES, pl.ds(step, SEGMENTS, stride=steps + BEFORE), :] = (
                gated[step, :, lanes] + query[step, :, lanes] * terms[0]
            )
            return tuple(decays[mode] * states[mode] for mode in range(modes))

        lax.fori_loop(0, steps, add, states, unroll=8)
    for group in range(channels // LANES):
        lanes = pl.ds(group * LANES, LANES)
        for out, block in ((keep, core), (send, 1 - core)):
            for segment in range(SEGMENTS // CORES):
                first = (block * (SEGMENTS // CORES) + segment) * (steps + BEFORE)
                first = pl.multiple_of(first, SEGMENTS)
                out[pl.ds(segment * steps, steps), lanes] = whole[
                    0, group, pl.ds(first, steps), :
                ].astype(jnp.bfloat16)


def carry_gated(where, query, gated, before, carried, decay, amplitude, power):
    steps, _, channels = query.shape
    length = steps * SEGMENTS // 2
    return pl.pallas_call(
        gate_kernel,
        out_shape=(jax.ShapeDtypeStruct((length, channels), jnp.bfloat16),) * 2,
        in_specs=[SMEM] + [VMEM] * 7,
        out_specs=(VMEM,) * 2,
        scratch_shapes=[segment_scratch(QUERY, 2 * length, channels)],
        compiler_params=pltpu.CompilerParams(vmem_limit_bytes=8 * 1024 * 1024),
        name="gated",
    )(where, *in_vmem(query, gated, before), carried, decay, amplitude, power)


def carry_factors(rate, x, z, span):
    x, z = x.astype(jnp.float32), z.astype(jnp.float32)

    def after(tokens):
        return jnp.exp(-rate * tokens)

    def if_before(position, steps):
        return jnp.where(position >= steps, 1.0, 0.0)

    line = [after(span * (Z - 1 - z))]
    for steps in range(1, Z):
        source = jnp.where(z >= steps, z - steps, z - steps + Z)
        line.append(after(span * (Z - 1 - source)))
    near = [if_before(z, steps) * after(float(span * (steps - 1))) for steps in range(1, Z)]
    far = [
        if_before(x, steps) * after(span * (Z * (steps - 1) + z)) for steps in range(1, X)
    ]
    return jnp.stack(line + near + far)


def carried_states(ends, factors):
    line, near, far = factors[:Z], factors[Z : 2 * Z - 1], factors[2 * Z - 1 :]
    others = [along_z(ends, steps) for steps in range(1, Z)]
    total, carry = line[0] * ends, 0.0
    for at, state in enumerate(others):
        total = total + line[at + 1] * state
        carry = carry + near[at] * state
    for at, state in enumerate([along_x(total, steps) for steps in range(1, X)]):
        carry = carry + far[at] * state
    return carry


def local(tokens, in_weight, short_filter, residues, rates, skip):
    index = lax.axis_index("seq")
    core = index % CORES
    z = index // CORES % Z
    x = index // (CORES * Z)
    where = jnp.stack([x, z, core]).astype(jnp.int32)
    length = tokens.shape[0]
    channels = skip.shape[0]
    half = channels // 2
    span = CORES * length
    first = core == 0

    def half_of(array, axis):
        return lax.dynamic_slice_in_dim(array, core * half, half, axis)

    low, high = in_weight[:, :, :half], in_weight[:, :, half:]
    received, later_tokens = together(swap_cores(jnp.where(first, high, low)), tokens)
    block = jnp.concatenate(
        [jnp.where(first, low, received), jnp.where(first, received, high)], axis=1
    )

    beside = across_z(block, 1)
    right, left = sides(block)
    other = swap_cores(later_tokens)
    held, late_tokens = together(block, later_tokens)
    tail = late_tokens[length - HALO :]
    held, other_tail = together(held, swap_cores(tail))
    over = across_z(held, 2)
    halo = next_chip(jnp.where(first, other_tail, tail))
    beside, right, left, other, *parameters = together(
        beside, right, left, other, rates, residues, short_filter, skip
    )
    rates, residues, short_filter, skip = parameters
    both = (tokens, other)

    rate = half_of(rates, 0).T
    residue = half_of(residues, 0).T
    decay = jnp.exp(-rate)
    amplitude = residue * jnp.sqrt(-jnp.expm1(-2.0 * rate))
    step = span // SEGMENTS
    power = jnp.stack([jnp.exp(-rate * (step * distance)) for distance in (1, 2, 4)])
    starts = jnp.arange(SEGMENTS, dtype=jnp.float32)[None, :, None] * step
    start_power = jnp.exp(-rate[:, None, :] * starts)
    factors = carry_factors(rate, x, z, span)
    taps = half_of(short_filter, 2)
    direct = half_of(skip, 0)[None, :]

    far = forwards(right, left)
    pieces = with_sides(0, block, right, left)
    products = partial_products(where, pieces, both, (halo,), (), "first")
    right, left = sides(beside)
    *far, over, products, halo_products = together(*far, over, *products)

    opposite = across_z(over, 1)
    far_beside = across_z(far[0], 1), across_z(far[1], 1)
    pieces = with_sides(1, beside, right, left) + with_far(0, *far)
    products = partial_products(
        where, pieces, both, (halo,), (products, halo_products), "second"
    )
    right, left = sides(over)
    right, left, products, halo_products = together(right, left, *products)

    pieces = with_sides(2, over, right, left)
    far = forwards(right, left)
    right, left = sides(opposite)
    far_opposite = across_z(far[0], 1), across_z(far[1], 1)
    pieces += with_sides(3, opposite) + with_far(2, *far)
    *products, rows = partial_products(
        where,
        pieces,
        both,
        (halo,),
        (products, halo_products),
        "third",
        ((1, 3), (3, 3), (2, 3), (2, 1)),
    )
    small = (power, start_power, factors, decay, amplitude, taps, direct)
    *last, products, halo_products, rows, power, start_power, factors, decay, amplitude, taps, direct = (
        together(right, left, *far_opposite, *far_beside, *products, rows, *small)
    )
    products = products, halo_products

    conv, before, ends = signals(
        rows, last, products, taps, decay, amplitude, power, direct
    )
    query, product = queries(rows, last, products, conv, taps)
    carried = carried_states(ends, factors)
    keep, send = carry_gated(
        where, query, product, before, carried, decay, amplitude, start_power
    )
    taken = swap_cores(send)
    return jnp.concatenate(
        [jnp.where(first, keep, taken), jnp.where(first, taken, keep)], axis=1
    )


def solution(mesh):
    placed = (
        P("seq", None),
        P(None, "seq", "mp"),
        P(None, None, "mp"),
        P("mp", None),
        P("mp", None),
        P("mp"),
    )
    return jax.shard_map(
        local, mesh=mesh, in_specs=placed, out_specs=P("seq", "mp"), check_vma=False
    )
```
